32 devices in a mesh: sample: 2 (over y), gx: 8 (over z, x), gy: 2 (over core).
Axes of the slice: x: 2, y: 2, z: 4, core: 2. Of those that a mesh axis runs over, the one named last changes fastest.
Arguments:
- displacement: float32 [2, 128, 1024], P(None, ('sample', 'gx'), 'gy'), parts along dimension 1, may hold values from -5 to 5
- velocity: float32 [2, 128, 1024], P(None, ('sample', 'gx'), 'gy'), parts along dimension 1, may hold values from -5 to 5
- pressure: float32 [128, 1024], P(('sample', 'gx'), 'gy'), parts along dimension 0, may hold values from -5 to 5
- broken_bits: int32 [10, 128, 1024], P(None, ('sample', 'gx'), 'gy'), parts along dimension 1, may hold values from 0 to 4095
- material_class: int32 [128, 1024], P(('sample', 'gx'), 'gy'), parts along dimension 0, may hold values from 0 to 3
- property_table: float32 [8, 4], P('sample'), parts along dimension 0, may hold values from 0.5 to 2
Outputs:
- final_displacement: float32 [2, 128, 1024], P(None, ('sample', 'gx'), 'gy'), parts along dimension 1
- final_velocity: float32 [2, 128, 1024], P(None, ('sample', 'gx'), 'gy'), parts along dimension 1
- final_pressure: float32 [128, 1024], P(('sample', 'gx'), 'gy'), parts along dimension 0
The draws below stay inside these ranges and needn't reach their ends.
There are 2 independent parts, one for each index of `sample`. The reference program is written for one: setup_inputs(seed, part) draws one part's arguments, and reference() takes and returns one part's arrays. A program takes and returns all parts, laid end to end along the dimension named above; each array names one. Nothing has to cross between parts.
Inputs may be any that keep to these rules, and one draw needn't show every extreme that they name: `broken_bits`: bits 12 and above of each word are 0.
All inputs are finite; a program needn't handle non-finite values.
Results may differ from the reference program's by a relative error of at most 0.00002.
Values sent between devices are 32-bit elements; how exact they have to be, the bound alone decides.
A program may use at most 64 MiB of HBM per device.

```python
import math
import jax
import jax.numpy as jnp

STEPS = 2
WORDS = 10
CLASSES = 4
NX = 64
NY = 1024


def touch_ends(array, rng, least, top_value):
    longest = array.shape.index(max(array.shape))
    spots = []
    for shift in (0, 1):
        where = [jax.random.randint(jax.random.fold_in(rng, axis), (), 0, length) for axis, length in enumerate(array.shape)]
        where[longest] = (where[longest] + shift) % array.shape[longest]
        spots.append(tuple(where))
    return array.at[spots[0]].set(least).at[spots[1]].set(top_value)


def block_scale(stream_key, dims, pieces, low, top_value):
    def one(dim, parts):
        heights = jax.random.uniform(jax.random.fold_in(jax.random.fold_in(stream_key, 6), dim), (parts,), jnp.float32, low / len(pieces), top_value / len(pieces))
        return jnp.repeat(jnp.exp(heights), dims[dim] // parts).reshape((-1,) + (1,) * (len(dims) - dim - 1))

    loudness = one(*pieces[0])
    for cut in pieces[1:]:
        loudness = loudness * one(*cut)
    return loudness


def noise(rng, extent, scale, reach, pieces=(), dtype=jnp.bfloat16):
    level = block_scale(rng, extent, pieces, -0.22, 0.18) if pieces else 1.0
    entries = jax.random.normal(rng, extent, jnp.float32) * scale * level
    return jnp.minimum(jnp.maximum(entries, -reach), reach).astype(dtype)


def setup_inputs(seed: int = 0, part: int = 0) -> dict:
    key_of = jax.random.split(jax.random.key(seed), 7)
    part_keys = jax.random.split(jax.random.fold_in(key_of[6], part), 7)
    return {
        "displacement": noise(part_keys[0], (2, NX, NY), 1.0, 5.0, ((1, 8), (2, 2)), jnp.float32),
        "velocity": noise(part_keys[1], (2, NX, NY), 1.0, 5.0, ((1, 8), (2, 2)), jnp.float32),
        "pressure": noise(part_keys[2], (NX, NY), 1.0, 5.0, ((0, 8), (1, 2)), jnp.float32),
        "broken_bits": touch_ends(jax.random.randint(part_keys[3], (WORDS, NX, NY), 0, 4096), jax.random.fold_in(part_keys[3], 1), 0, 4095).astype(jnp.int32),
        "material_class": touch_ends(jax.random.randint(part_keys[4], (NX, NY), 0, CLASSES), jax.random.fold_in(part_keys[4], 1), 0, CLASSES - 1).astype(jnp.int32),
        "property_table": jnp.clip(jnp.exp(jax.random.uniform(part_keys[5], (CLASSES, 4), jnp.float32, math.log(0.5), math.log(2.0))), 0.5, 2.0),
    }


bond_offsets = [(row_step, col_step) for row_step in range(-6, 7) for col_step in range(-6, 7) if 0 < row_step * row_step + col_step * col_step <= 37]

def material_of(material_class, property_table):
    material = jnp.zeros((4,) + material_class.shape, jnp.float32)
    for klass in range(property_table.shape[0]):
        chosen = jnp.where(material_class == klass, 1.0, 0.0).astype(jnp.float32)
        material = material + chosen[None] * property_table[klass][:, None, None]
    return material

def advance(padded, fields, padded_material, material, broken_bits, velocity):
    height, breadth = (fields.shape[1], fields.shape[2])
    force_x = jnp.zeros((height, breadth), jnp.float32)
    force_y = jnp.zeros((height, breadth), jnp.float32)
    dilation = jnp.zeros((height, breadth), jnp.float32)
    inflow = jnp.zeros((height, breadth), jnp.float32)
    for bond_index, (row_step, col_step) in enumerate(bond_offsets):
        beyond = padded[:, 6 + row_step:6 + row_step + height, 6 + col_step:6 + col_step + breadth]
        other = padded_material[:, 6 + row_step:6 + row_step + height, 6 + col_step:6 + col_step + breadth]
        length = math.sqrt(row_step * row_step + col_step * col_step)
        word = broken_bits[bond_index // 12]
        intact = (1 - jnp.bitwise_and(jnp.right_shift(word, bond_index % 12), 1)).astype(jnp.float32)
        stretch = (row_step * (beyond[0] - fields[0]) + col_step * (beyond[1] - fields[1])) / (length * length)
        bond_stiff = 2.0 * material[0] * other[0] / (material[0] + other[0])
        bond_perm = 2.0 * material[1] * other[1] / (material[1] + other[1])
        magnitude = intact * bond_stiff * (stretch - 0.5 * (fields[2] + beyond[2]) * 0.5) / length
        force_x = force_x + magnitude * (row_step / length)
        force_y = force_y + magnitude * (col_step / length)
        dilation = dilation + intact * bond_stiff * stretch / length
        inflow = inflow + intact * bond_perm * (beyond[2] - fields[2]) / (length * length)
    force = jnp.stack([force_x, force_y])
    new_velocity = velocity + 0.1 * (material[2][None] * force - 0.5 * velocity)
    new_displacement = fields[:2] + 0.1 * new_velocity
    new_pressure = fields[2] + 0.1 * material[3] * 0.1 * (inflow - dilation)
    return (new_displacement, new_velocity, new_pressure)

def reference(displacement, velocity, pressure, broken_bits, material_class, property_table):
    material = material_of(material_class, property_table)
    padded_material = jnp.pad(material, ((0, 0), (6, 6), (6, 6)))
    for iteration in range(STEPS):
        fields = jnp.concatenate([displacement, pressure[None]], axis=0)
        padded = jnp.pad(fields, ((0, 0), (6, 6), (6, 6)))
        displacement, velocity, pressure = advance(padded, fields, padded_material, material, broken_bits, velocity)
    return (displacement, velocity, pressure)
```

```python
import functools
import math

import jax
import jax.numpy as jnp
from jax import lax
from jax.experimental import pallas as pl
from jax.experimental.pallas import tpu as pltpu
from jax.sharding import PartitionSpec as P

REACH = 6
SPAN = 2 * REACH + 1
MESH = pl.DeviceIdType.MESH
LANES = 128
ROWS = 8
OUTSIDE = -1
FAR = 3.0e38

half_width = {a: math.isqrt(37 - a * a) for a in range(-REACH, REACH + 1)}
first_bond = {}
_count = 0
for _a in range(-REACH, REACH + 1):
    first_bond[_a] = _count
    _count += 2 * half_width[_a] + 1 - (1 if _a == 0 else 0)


def bond(a, b):
    if abs(a) > REACH or abs(b) > half_width[a] or (a == 0 and b == 0):
        return None
    return first_bond[a] + b + half_width[a] - (1 if a == 0 and b > 0 else 0)


def groups_of(own):
    out = [(0, 0, 0)] if own else []
    for o in range(1, ROWS):
        out.append((o, o, o - ROWS) if own else (o, o - ROWS, o))
    return out


def columns_of(low, high):
    return max(half_width.get(low, -1), half_width.get(high, -1))


def slots_of(own):
    slots = {}
    for o, low, high in groups_of(own):
        for b in range(-columns_of(low, high), columns_of(low, high) + 1):
            if (o, b) != (0, 0):
                slots[o, b] = len(slots)
    return slots


SLOTS = {own: slots_of(own) for own in (True, False)}


def kernel(
    gx_count, disp, vel, pres, bits, klass, table,
    out_disp, out_vel, out_pres,
    disp_v, vel_v, pres_v, bits_v, klass_v, table_s,
    own1, far1, own2, far2,
    z_own, z_far, q_own, q_far, inv_own, inv_far, inverse, here_inv,
    w_own, v_own, w_far, v_far, ex_far, side_b, still,
    local_sem, send_sem, recv_sem, send2_sem, recv2_sem,
):
    f32 = jnp.float32
    sample, gx, gy = lax.axis_index("sample"), lax.axis_index("gx"), lax.axis_index("gy")
    height, breadth = pres.shape
    blocks = breadth // LANES
    has_up, has_down = gx > 0, gx < gx_count - 1
    up, down, mate = gx - 1, gx + 1, 1 - gy

    local = [
        pltpu.make_async_copy(table, table_s, local_sem.at[0]),
        pltpu.make_async_copy(klass, klass_v, local_sem.at[1]),
        pltpu.make_async_copy(disp, disp_v, local_sem.at[2]),
        pltpu.make_async_copy(pres, pres_v, local_sem.at[3]),
        pltpu.make_async_copy(bits, bits_v, local_sem.at[4]),
        pltpu.make_async_copy(vel, vel_v, local_sem.at[5]),
    ]
    for copy in local:
        copy.start()

    for plane in range(4):
        fill = float(OUTSIDE) if plane == 3 else 0.0
        far1[plane] = jnp.full(far1.shape[1:], fill, f32)
        if plane < 3:
            far2[plane] = jnp.zeros(far2.shape[1:], f32)

    barrier = pltpu.get_barrier_semaphore()

    def greet(x, y):
        pl.semaphore_signal(barrier, inc=1, device_id=(sample, x, y), device_id_type=MESH)

    @pl.when(has_up)
    def _():
        greet(up, gy)
        greet(up, mate)

    @pl.when(has_down)
    def _():
        greet(down, gy)
        greet(down, mate)

    greet(gx, mate)

    def cut(value):
        return [value[:, j * LANES : (j + 1) * LANES] for j in range(blocks)]

    def put(target, plane, value):
        for j, piece in enumerate(cut(value)):
            for rows in (slice(0, ROWS), slice(ROWS, 2 * ROWS)):
                target[plane, j, rows, :] = piece

    for i in (1, 2, 3):
        local[i].wait()
    put(own1, 3, klass_v[...].astype(f32))
    put(own1, 0, disp_v[0])
    put(own1, 1, disp_v[1])
    put(own1, 2, pres_v[...])

    sides = pl.ds(0, blocks)
    edge, rim = pl.ds((1 - gy) * (blocks - 1), 1), pl.ds(blocks, 1)
    to_up = (pl.ds(0, REACH), pl.ds(ROWS, REACH))
    to_down = (pl.ds(ROWS - REACH, REACH), pl.ds(ROWS - REACH, REACH))
    routes = (
        (has_up, has_down, (sample, up, gy), to_up, True),
        (has_down, has_up, (sample, down, gy), to_down, True),
        (has_up, has_down, (sample, up, mate), to_up, False),
        (has_down, has_up, (sample, down, mate), to_down, False),
        (None, None, (sample, gx, mate), None, False),
    )

    def when(condition, act):
        if condition is None:
            act()
        else:
            pl.when(condition)(act)

    def exchange(own, far, sends, recvs):
        copies = []
        for n, (_, _, device, rows, whole) in enumerate(routes):
            here, land = (sides, sides) if whole else (edge, rim)
            if rows is None:
                source, target = own.at[:, here, pl.ds(0, ROWS)], own.at[:, land, pl.ds(0, ROWS)]
            else:
                source, target = own.at[:, here, rows[0]], far.at[:, land, rows[1]]
            copies.append(
                pltpu.make_async_remote_copy(
                    src_ref=source, dst_ref=target, send_sem=sends.at[n], recv_sem=recvs.at[n],
                    device_id=device, device_id_type=MESH,
                )
            )
        return copies

    def start(copies):
        for n, copy in enumerate(copies):
            when(routes[n][0], copy.start)

    def arrive(copies, which):
        for n in which:
            when(routes[n][1], copies[n].wait_recv)

    pl.semaphore_wait(
        barrier, 1 + 2 * has_up.astype(jnp.int32) + 2 * has_down.astype(jnp.int32)
    )
    first = exchange(own1, far1, send_sem, recv_sem)
    start(first)

    sublane = lax.broadcasted_iota(jnp.int32, (ROWS, LANES), 0)
    lane = lax.broadcasted_iota(jnp.int32, (ROWS, LANES), 1)

    def mix(o, low, high, kind=f32):
        return kind(low) if low == high else jnp.where(sublane < ROWS - o, kind(low), kind(high))

    local[0].wait()

    def look_up(which, member):
        value = jnp.full(which.shape, table_s[table.shape[0] - 1, member], f32)
        for c in range(table.shape[0] - 1):
            value = jnp.where(which == c, table_s[c, member], value)
        return value

    classes = table.shape[0]
    for m in range(2):
        for c in range(classes):
            inverse[m, c] = 1.0 / jnp.full((ROWS, LANES), table_s[c, m], f32)

    def inverses(which):
        out = [jnp.full(which.shape, FAR, f32)] * 2
        for c in range(classes):
            chosen = which == float(c)
            out = [jnp.where(chosen, inverse[m, c], out[m]) for m in range(2)]
        return out

    for m, value in enumerate(inverses(own1[3, :blocks, 0:ROWS, :])):
        here_inv[m] = value

    klass_own = klass_v[...]
    for plane, member in ((0, 2), (1, 3)):
        for j, piece in enumerate(cut(look_up(klass_own, member))):
            still[plane, j] = piece
    local[4].wait()
    for j in range(blocks):
        words = [bits_v[w, :, j * LANES : (j + 1) * LANES] for w in range(bits.shape[0])]

        def broken(a, b):
            k = bond(a, b)
            return jnp.int32(1) if k is None else words[k // 12] & (1 << (k % 12))

        for own, w_to, v_to in ((True, w_own, v_own), (False, w_far, v_far)):
            for o, low, high in groups_of(own):
                for b in range(-columns_of(low, high), columns_of(low, high) + 1):
                    if (o, b) not in SLOTS[own]:
                        continue
                    n = SLOTS[own][o, b]
                    one = broken(low, b)
                    if o:
                        one = jnp.where(sublane < ROWS - o, one, broken(high, b))
                    squares = [a * a + b * b for a in (low, high)]
                    w_to[n, j] = jnp.where(one == 0, mix(o, *[2.0 / x**2 for x in squares]), 0.0)
                    v_to[n, j] = jnp.where(one == 0, mix(o, *[2.0 / x for x in squares]), 0.0)

    def shift(value, b):
        if b == 0:
            return value[:blocks]
        turned = pltpu.roll(value, (-b) % LANES, 2)
        if b > 0:
            return jnp.where(lane < LANES - b, turned[:blocks], turned[1:])
        before = jnp.concatenate([turned[blocks:], turned[: blocks - 1]], axis=0)
        return jnp.where(lane >= -b, turned[:blocks], before)

    def tiles(own):
        top, bottom = slice(0, ROWS), slice(ROWS, 2 * ROWS)
        return [(top, (top, bottom))] if own else [(top, (top,)), (bottom, (bottom,))]

    valid = (lane < LANES // 2) == (gy == 0)

    def materials(own, x, target):
        for read, write in tiles(own):
            value = x[3, :, read, :]
            rim_value = jnp.where(valid, value[blocks:], float(OUTSIDE))
            value = jnp.concatenate([value[:blocks], rim_value], axis=0)
            for m, value in enumerate(inverses(value)):
                for b in range(-REACH, REACH + 1):
                    moved = shift(value, b)
                    for rows in write:
                        target[m, b + REACH, :, rows, :] = moved

    def prepare(own, x, z, q_moved):
        for read, write in tiles(own):
            v, q = x[1, :, read, :], x[2, :, read, :]
            for b in range(-REACH, REACH + 1):
                moved = shift(q, b)
                for rows in write:
                    q_moved[b + REACH, :, rows, :] = moved
            for b in range(1, REACH + 1):
                bv, bq = float(b) * v, (-0.25 * b * b) * q
                for rows in write:
                    z[REACH + b, :, rows, :] = bq + bv
                    z[REACH - b, :, rows, :] = bq - bv

    def centre(x):
        v, p = x[1, :blocks, 0:ROWS, :], x[2, :blocks, 0:ROWS, :]
        for b in range(-REACH, REACH + 1):
            if b:
                side_b[b + REACH] = float(b) * v + (0.25 * b * b) * p

    def row_centre(x, o, low, high):
        u, p = x[0, :blocks, 0:ROWS, :], x[2, :blocks, 0:ROWS, :]
        return mix(o, low, high) * u + mix(o, 0.25 * low * low, 0.25 * high * high) * p

    def centre_far(x):
        for o, low, high in groups_of(False):
            here = row_centre(x, o, low, high)
            for b in range(-columns_of(low, high), columns_of(low, high) + 1):
                n = SLOTS[False][o, b]
                ex_far[n] = here if b == 0 else here + side_b[b + REACH]

    def evaluate(own, x, z, q_moved, sums, fresh):
        w_ref, v_ref = (w_own, v_own) if own else (w_far, v_far)
        inv = inv_own if own else inv_far
        slots = SLOTS[own]
        force_x, force_y, gain, drain = sums
        for o, low, high in groups_of(own):
            rows = pl.ds(o, ROWS)
            wide = columns_of(low, high)
            if o:
                y = (
                    mix(o, low, high) * x[0, :, rows, :]
                    - mix(o, 0.25 * low * low, 0.25 * high * high) * x[2, :, rows, :]
                )
            if own and o:
                here = row_centre(x, o, low, high)
            row_sum = None

            def one(b):
                n = slots[o, b]
                if fresh:
                    cubes = [0.25 * math.sqrt(a * a + b * b) ** 3 for a in (low, high)]
                    weight, flow = (
                        ref[n]
                        * pl.reciprocal(
                            here_inv[m] + inv[m, b + REACH, :, rows, :], approx=True
                        )
                        for m, ref in enumerate((w_ref, v_ref))
                    )
                    share = mix(o, *cubes) * weight
                    lost, flow = flow + share, flow - share
                    w_ref[n] = weight
                    v_ref[n] = flow
                else:
                    weight, flow, lost = w_ref[n], v_ref[n], None
                if b == 0:
                    there = y[:blocks]
                else:
                    there = z[b + REACH, :, rows, :]
                    there = shift(y + there if o else there, b)
                if not own:
                    mine = ex_far[n]
                elif o == 0:
                    mine = side_b[b + REACH]
                else:
                    mine = here if b == 0 else here + side_b[b + REACH]
                mag = weight * (there - mine)
                return mag, flow * q_moved[b + REACH, :, rows, :], lost

            for b in range(wide + 1):
                if (o, b) not in slots:
                    continue
                length = mix(o, *[math.sqrt(a * a + b * b) for a in (low, high)])
                mag, flow, lost = one(b)
                gain = gain + flow
                if fresh:
                    drain = drain + lost
                if b:
                    mag2, flow, lost = one(-b)
                    gain = gain + flow
                    if fresh:
                        drain = drain + lost
                    force_y = force_y + float(b) * (mag - mag2)
                    mag = mag + mag2
                gain = gain - length * mag
                row_sum = mag if row_sum is None else row_sum + mag
            if o:
                force_x = force_x + mix(o, low, high) * row_sum
        return force_x, force_y, gain, drain

    def duplicate_rim(x, planes):
        for plane in range(planes):
            x[plane, blocks, ROWS : 2 * ROWS, :] = x[plane, blocks, 0:ROWS, :]

    def half_step(x, z, q, sums, fresh):
        prepare(True, x, z, q)
        centre(x)
        centre_far(x)
        return evaluate(True, x, z, q, sums, fresh)

    def finish(x, sums, drain, velocity):
        force_x, force_y, gain, _ = sums
        u0, u1, p = (x[plane, :blocks, 0:ROWS, :] for plane in range(3))
        density, storage = still[0], still[1]
        v0 = velocity[0] + 0.1 * (density * force_x - 0.5 * velocity[0])
        v1 = velocity[1] + 0.1 * (density * force_y - 0.5 * velocity[1])
        pressure = p + 0.1 * storage * 0.1 * (gain - drain * p)
        return u0 + 0.1 * v0, u1 + 0.1 * v1, pressure, v0, v1

    zero = jnp.zeros((blocks, ROWS, LANES), f32)

    arrive(first, (4,))
    duplicate_rim(own1, 4)
    materials(True, own1, inv_own)
    sums = half_step(own1, z_own, q_own, (zero,) * 4, True)
    local[5].wait()
    velocity = [jnp.stack(cut(vel_v[i])) for i in range(2)]

    arrive(first, (0, 1, 2, 3))
    materials(False, far1, inv_far)
    prepare(False, far1, z_far, q_far)
    sums = evaluate(False, far1, z_far, q_far, sums, True)
    drain = sums[3]
    n0, n1, np_, v0, v1 = finish(own1, sums, drain, velocity)
    for plane, value in enumerate((n0, n1, np_)):
        own2[plane, :blocks, 0:ROWS, :] = value
        own2[plane, :blocks, ROWS : 2 * ROWS, :] = value

    second = exchange(own2, far2, send2_sem, recv2_sem)
    start(second)
    arrive(second, (4,))
    duplicate_rim(own2, 3)
    sums = half_step(own2, z_own, q_own, (zero,) * 4, False)
    arrive(second, (0, 1, 2, 3))
    prepare(False, far2, z_far, q_far)
    sums = evaluate(False, far2, z_far, q_far, sums, False)
    n0, n1, np_, v0, v1 = finish(own2, sums, drain, (v0, v1))

    for j in range(blocks):
        at = slice(j * LANES, (j + 1) * LANES)
        out_disp[0, :, at] = n0[j]
        out_disp[1, :, at] = n1[j]
        out_vel[0, :, at] = v0[j]
        out_vel[1, :, at] = v1[j]
        out_pres[:, at] = np_[j]

    for copies in (first, second):
        for n, copy in enumerate(copies):
            when(routes[n][0], copy.wait_send)


def hand_over(a, b, c, out_a, out_b, out_c, sems):
    copies = [
        pltpu.make_async_copy(source, target, sems.at[i])
        for i, (source, target) in enumerate(((a, out_a), (b, out_b), (c, out_c)))
    ]
    for copy in copies:
        copy.start()
    for copy in copies:
        copy.wait()


def body(gx_count, displacement, velocity, pressure, broken_bits, material_class, table):
    height, breadth = pressure.shape
    assert height == ROWS and breadth % LANES == 0 and breadth // LANES > 1
    blocks = breadth // LANES
    vmem = pl.BlockSpec(memory_space=pltpu.VMEM)
    anywhere = pl.BlockSpec(memory_space=pltpu.HBM)
    f, i32 = jnp.float32, jnp.int32
    dma = pltpu.SemaphoreType.DMA
    n_own, n_far = (len(SLOTS[own]) for own in (True, False))

    def planes(n, blocks, rows):
        return pltpu.VMEM((n, blocks, rows, LANES), f)

    shapes = (displacement.shape, velocity.shape, pressure.shape)
    results = pl.pallas_call(
        functools.partial(kernel, gx_count),
        out_shape=tuple(pltpu.VMEM(s, f) for s in shapes),
        in_specs=[anywhere] * 6,
        out_specs=(vmem, vmem, vmem),
        scratch_shapes=[
            pltpu.VMEM(displacement.shape, f),
            pltpu.VMEM(velocity.shape, f),
            pltpu.VMEM(pressure.shape, f),
            pltpu.VMEM(broken_bits.shape, i32),
            pltpu.VMEM(material_class.shape, i32),
            pltpu.SMEM(table.shape, f),
            planes(4, blocks + 1, 2 * ROWS),
            planes(4, blocks + 1, 2 * ROWS),
            planes(3, blocks + 1, 2 * ROWS),
            planes(3, blocks + 1, 2 * ROWS),
            planes(SPAN, blocks + 1, 2 * ROWS),
            planes(SPAN, blocks + 1, 2 * ROWS),
            planes(SPAN, blocks, 2 * ROWS),
            planes(SPAN, blocks, 2 * ROWS),
            pltpu.VMEM((2, SPAN, blocks, 2 * ROWS, LANES), f),
            pltpu.VMEM((2, SPAN, blocks, 2 * ROWS, LANES), f),
            planes(2, table.shape[0], ROWS),
            planes(2, blocks, ROWS),
            planes(n_own, blocks, ROWS),
            planes(n_own, blocks, ROWS),
            planes(n_far, blocks, ROWS),
            planes(n_far, blocks, ROWS),
            planes(n_far, blocks, ROWS),
            planes(SPAN, blocks, ROWS),
            planes(2, blocks, ROWS),
            dma((6,)), dma((5,)), dma((5,)), dma((5,)), dma((5,)),
        ],
        compiler_params=pltpu.CompilerParams(
            collective_id=0, has_side_effects=True, vmem_limit_bytes=62 * 1024 * 1024
        ),
        name="peridynamics",
    )(displacement, velocity, pressure, broken_bits, material_class, table)
    return pl.pallas_call(
        hand_over,
        out_shape=tuple(jax.ShapeDtypeStruct(s, f) for s in shapes),
        in_specs=[vmem] * 3,
        out_specs=(anywhere,) * 3,
        scratch_shapes=[dma((3,))],
        name="hand_over",
    )(*[pltpu.with_memory_space_constraint(r, pltpu.VMEM) for r in results])


def solution(mesh):
    plane = P(("sample", "gx"), "gy")
    stack = P(None, ("sample", "gx"), "gy")
    assert mesh.shape["gy"] == 2
    return jax.shard_map(
        functools.partial(body, mesh.shape["gx"]),
        mesh=mesh,
        in_specs=(stack, stack, plane, stack, plane, P("sample", None)),
        out_specs=(stack, stack, plane),
        check_vma=False,
    )
```

```python
import functools
import math

import jax
import jax.numpy as jnp
from jax import lax
from jax.experimental import pallas as pl
from jax.experimental.pallas import tpu as pltpu
from jax.sharding import PartitionSpec as P

REACH = 6
SPAN = 2 * REACH + 1
MESH = pl.DeviceIdType.MESH
LANES = 128
ROWS = 8
OUTSIDE = -1
PLACES = (0, 3, 1, 2)
RIM = len(PLACES)
AFTER, BEFORE = (2, RIM, 3, 1), (RIM, 3, 0, 2)
OUTER, INNER, ALL = (0, 1), (2, 3), (0, 1, 2, 3)
MESSAGES = 17
HALF = 4
FAR = 3.0e38

half_width = {a: math.isqrt(37 - a * a) for a in range(-REACH, REACH + 1)}
first_bond = {}
_count = 0
for _a in range(-REACH, REACH + 1):
    first_bond[_a] = _count
    _count += 2 * half_width[_a] + 1 - (1 if _a == 0 else 0)


def bond(a, b):
    if abs(a) > REACH or abs(b) > half_width[a] or (a == 0 and b == 0):
        return None
    return first_bond[a] + b + half_width[a] - (1 if a == 0 and b > 0 else 0)


def groups_of(own):
    out = [(0, 0, 0)] if own else []
    for o in range(1, ROWS):
        out.append((o, o, o - ROWS) if own else (o, o - ROWS, o))
    return out


def columns_of(low, high):
    return max(half_width.get(low, -1), half_width.get(high, -1))


def slots_of(own):
    slots = {}
    for o, low, high in groups_of(own):
        for b in range(-columns_of(low, high), columns_of(low, high) + 1):
            if (o, b) != (0, 0):
                slots[o, b] = len(slots)
    return slots


SLOTS = {own: slots_of(own) for own in (True, False)}


def kernel(
    gx_count, disp, vel, pres, bits, klass, table,
    out_disp, out_vel, out_pres,
    disp_v, vel_v, pres_v, bits_v, klass_v, table_s,
    own1, far1, own2, far2,
    z_own, z_far, q_own, q_far, inv_own, inv_far, inverse, here_inv,
    w_own, v_own, w_far, v_far, ex_own, ex_far, y_own, y_far, side_b, still,
    local_sem, send_sem, recv_sem,
):
    f32 = jnp.float32
    sample, gx, gy = lax.axis_index("sample"), lax.axis_index("gx"), lax.axis_index("gy")
    height, breadth = pres.shape
    blocks = breadth // LANES
    has_up, has_down = gx > 0, gx < gx_count - 1
    up, down, mate = gx - 1, gx + 1, 1 - gy

    local = [
        pltpu.make_async_copy(table, table_s, local_sem.at[0]),
        pltpu.make_async_copy(klass, klass_v, local_sem.at[1]),
        pltpu.make_async_copy(disp, disp_v, local_sem.at[2]),
        pltpu.make_async_copy(pres, pres_v, local_sem.at[3]),
        pltpu.make_async_copy(bits, bits_v, local_sem.at[4]),
        pltpu.make_async_copy(vel, vel_v, local_sem.at[5]),
    ]
    for copy in local:
        copy.start()

    for plane in range(4):
        fill = float(OUTSIDE) if plane == 3 else 0.0
        far1[plane] = jnp.full(far1.shape[1:], fill, f32)
        if plane < 3:
            far2[plane] = jnp.zeros(far2.shape[1:], f32)

    barrier = pltpu.get_barrier_semaphore()

    def greet(x, y):
        pl.semaphore_signal(barrier, inc=1, device_id=(sample, x, y), device_id_type=MESH)

    @pl.when(has_up)
    def _():
        greet(up, gy)
        greet(up, mate)

    @pl.when(has_down)
    def _():
        greet(down, gy)
        greet(down, mate)

    greet(gx, mate)

    def cut(value):
        return [value[:, j * LANES : (j + 1) * LANES] for j in PLACES]

    def put(target, plane, value):
        for j, piece in enumerate(cut(value)):
            for rows in (slice(0, ROWS), slice(ROWS, 2 * ROWS)):
                target[plane, j, rows, :] = piece

    for i in (1, 2, 3):
        local[i].wait()
    put(own1, 3, klass_v[...].astype(f32))
    put(own1, 0, disp_v[0])
    put(own1, 1, disp_v[1])
    put(own1, 2, pres_v[...])

    edge, rim = pl.ds(1 - gy, 1), pl.ds(RIM, 1)
    to_up = (pl.ds(0, REACH), pl.ds(ROWS, REACH))
    to_down = (pl.ds(ROWS - REACH, REACH), pl.ds(ROWS - REACH, REACH))
    routes = (
        (has_up, has_down, (sample, up, gy), to_up),
        (has_down, has_up, (sample, down, gy), to_down),
        (has_up, has_down, (sample, up, mate), to_up),
        (has_down, has_up, (sample, down, mate), to_down),
        (None, None, (sample, gx, mate), None),
    )
    STRAIGHT, CORNERS, ACROSS = (0, 1), (2, 3), (4,)
    messages = []

    def when(condition, act):
        if condition is None:
            act()
        else:
            pl.when(condition)(act)

    def send(own, far, planes, which, blocks=None):
        sent = []
        for n in which:
            going, coming, device, rows = routes[n]
            here, land = (edge, rim) if blocks is None else (blocks, blocks)
            if rows is None:
                source = own.at[planes, here, pl.ds(0, ROWS)]
                target = own.at[planes, land, pl.ds(0, ROWS)]
            else:
                source = own.at[planes, here, rows[0]]
                target = far.at[planes, land, rows[1]]
            m = len(messages)
            copy = pltpu.make_async_remote_copy(
                src_ref=source, dst_ref=target, send_sem=send_sem.at[m], recv_sem=recv_sem.at[m],
                device_id=device, device_id_type=MESH,
            )
            when(going, copy.start)
            messages.append((going, copy))
            sent.append((coming, copy))
        return sent

    waited = []

    def finish_sends(count):
        for going, copy in messages[len(waited) : count]:
            when(going, copy.wait_send)
            waited.append(copy)

    def arrive(sent):
        for coming, copy in sent:
            when(coming, copy.wait_recv)

    pl.semaphore_wait(
        barrier, 1 + 2 * has_up.astype(jnp.int32) + 2 * has_down.astype(jnp.int32)
    )
    fields, kinds = pl.ds(0, 3), pl.ds(3, 1)
    four = pl.ds(0, blocks)
    kinds_far = send(own1, far1, kinds, STRAIGHT, four) + send(own1, far1, kinds, CORNERS)
    kinds_rim = send(own1, far1, kinds, ACROSS)
    fields_far = send(own1, far1, fields, STRAIGHT, four) + send(own1, far1, fields, CORNERS)
    fields_rim = send(own1, far1, fields, ACROSS)

    sublane = lax.broadcasted_iota(jnp.int32, (ROWS, LANES), 0)
    lane = lax.broadcasted_iota(jnp.int32, (ROWS, LANES), 1)

    def mix(o, low, high, kind=f32):
        return kind(low) if low == high else jnp.where(sublane < ROWS - o, kind(low), kind(high))

    local[0].wait()

    def look_up(which, member):
        value = jnp.full(which.shape, table_s[table.shape[0] - 1, member], f32)
        for c in range(table.shape[0] - 1):
            value = jnp.where(which == c, table_s[c, member], value)
        return value

    classes = table.shape[0]
    for m in range(2):
        for c in range(classes):
            inverse[m, c] = 1.0 / jnp.full((ROWS, LANES), table_s[c, m], f32)

    def inverses(which):
        out = [jnp.full(which.shape, FAR, f32)] * 2
        for c in range(classes):
            chosen = which == float(c)
            out = [jnp.where(chosen, inverse[m, c], out[m]) for m in range(2)]
        return out

    for m, value in enumerate(inverses(own1[3, :blocks, 0:ROWS, :])):
        here_inv[m] = value

    klass_own = klass_v[...]
    for plane, member in ((0, 2), (1, 3)):
        for j, piece in enumerate(cut(look_up(klass_own, member))):
            still[plane, j] = piece
    local[4].wait()
    for j in range(blocks):
        words = [bits_v[w, :, PLACES[j] * LANES : (PLACES[j] + 1) * LANES] for w in range(bits.shape[0])]

        def broken(a, b):
            k = bond(a, b)
            return jnp.int32(1) if k is None else words[k // 12] & (1 << (k % 12))

        for own, w_to, v_to in ((True, w_own, v_own), (False, w_far, v_far)):
            for o, low, high in groups_of(own):
                for b in range(-columns_of(low, high), columns_of(low, high) + 1):
                    if (o, b) not in SLOTS[own]:
                        continue
                    n = SLOTS[own][o, b]
                    one = broken(low, b)
                    if o:
                        one = jnp.where(sublane < ROWS - o, one, broken(high, b))
                    squares = [a * a + b * b for a in (low, high)]
                    w_to[n, j] = jnp.where(one == 0, mix(o, *[2.0 / x**2 for x in squares]), 0.0)
                    v_to[n, j] = jnp.where(one == 0, mix(o, *[2.0 / x for x in squares]), 0.0)

    def load(get, which):
        runs = []
        for k in which:
            if runs and runs[-1][1] == k:
                runs[-1][1] = k + 1
            else:
                runs.append([k, k + 1])
        pieces = [get(*run) for run in runs]
        return pieces[0] if len(pieces) == 1 else jnp.concatenate(pieces, axis=0)

    def shift(get, b, outs=ALL):
        if b == 0:
            return load(get, outs)
        other = [(AFTER if b > 0 else BEFORE)[k] for k in outs]
        sources = sorted(set(outs) | set(other))
        turned = pltpu.roll(load(get, sources), (-b) % LANES, 2)

        def take(which):
            at = [sources.index(k) for k in which]
            return load(lambda i, j: turned[i:j], at)

        return jnp.where(lane < LANES - b if b > 0 else lane >= -b, take(outs), take(other))

    def tiles(own):
        top, bottom = slice(0, ROWS), slice(ROWS, 2 * ROWS)
        return [(top, (top, bottom))] if own else [(top, (top,)), (bottom, (bottom,))]

    valid = (lane < LANES // 2) == (gy == 0)

    def weigh(own, x):
        w_ref, v_ref, inv = (w_own, v_own, inv_own) if own else (w_far, v_far, inv_far)
        known = []
        for read, write in tiles(own):
            value = x[3, :, read, :]
            rim_value = jnp.where(valid, value[blocks:], float(OUTSIDE))
            known.append(inverses(jnp.concatenate([value[:blocks], rim_value], axis=0)))
        drain = jnp.zeros((blocks, ROWS, LANES), f32)
        for b in sorted(range(-REACH, REACH + 1), key=abs):
            for (read, write), pair in zip(tiles(own), known):
                for m, value in enumerate(pair):
                    moved = shift(lambda i, j: value[i:j], b)
                    for rows in write:
                        inv[m, b + REACH, :, rows, :] = moved
            for o, low, high in groups_of(own):
                if (o, b) not in SLOTS[own]:
                    continue
                n = SLOTS[own][o, b]
                cubes = [0.25 * math.sqrt(a * a + b * b) ** 3 for a in (low, high)]
                weight, flow = (
                    ref[n]
                    * pl.reciprocal(
                        here_inv[m] + inv[m, b + REACH, :, pl.ds(o, ROWS), :], approx=True
                    )
                    for m, ref in enumerate((w_ref, v_ref))
                )
                share = mix(o, *cubes) * weight
                w_ref[n] = weight
                v_ref[n] = flow - share
                drain = drain + (flow + share)
        return drain

    def centre(x):
        u, v, p = (x[plane, :blocks, 0:ROWS, :] for plane in range(3))
        for b in range(-REACH, REACH + 1):
            side_b[b + REACH] = float(b) * v + (0.25 * b * b) * p
        for own, target in ((True, ex_own), (False, ex_far)):
            for o, low, high in groups_of(own):
                here = mix(o, low, high) * u + mix(o, 0.25 * low * low, 0.25 * high * high) * p
                for b in range(-columns_of(low, high), columns_of(low, high) + 1):
                    if (o, b) in SLOTS[own]:
                        target[SLOTS[own][o, b]] = here if b == 0 else here + side_b[b + REACH]

    def evaluate(own, x, sums, outs=ALL, ready=False, ends="both"):
        w_ref, v_ref, ex, z, q_moved, y = (
            (w_own, v_own, ex_own, z_own, q_own, y_own)
            if own
            else (w_far, v_far, ex_far, z_far, q_far, y_far)
        )
        slots = SLOTS[own]
        force_x, force_y, gain = sums
        span = slice(outs[0], outs[-1] + 1)
        ready = ready or ends == "near"
        if not ready:
            for o, low, high in groups_of(own):
                if o:
                    rows = pl.ds(o, ROWS)
                    y[o - 1] = (
                        mix(o, low, high) * x[0, :, rows, :]
                        - mix(o, 0.25 * low * low, 0.25 * high * high) * x[2, :, rows, :]
                    )
        groups = groups_of(own)
        sets = (groups,) if len(outs) < len(ALL) else (groups[: HALF], groups[HALF:])
        for chosen in sets:
            row_sums = {}
            for b in range(REACH + 1):
                if not ready and chosen is sets[0]:
                    for read, write in tiles(own):
                        if b:
                            v, q = x[1, :, read, :], x[2, :, read, :]
                            bv, bq = float(b) * v, (-0.25 * b * b) * q
                            for rows in write:
                                z[REACH + b, :, rows, :] = bq + bv
                                z[REACH - b, :, rows, :] = bq - bv
                        for c in (b, -b) if b else (0,):
                            moved = shift(lambda i, j: x[2, i:j, read, :], c)
                            for rows in write:
                                q_moved[c + REACH, :, rows, :] = moved
                side_sum = None
                for o, low, high in chosen:
                    if (o, b) not in slots:
                        continue
                    rows = pl.ds(o, ROWS)

                    def one(c):
                        n = slots[o, c]

                        def there(i, j):
                            if c == 0:
                                return y[o - 1, i:j]
                            side = z[c + REACH, i:j, rows, :]
                            return side + y[o - 1, i:j] if o else side

                        if ends == "near":
                            return w_ref[n, span] * ex[n, span], None
                        far = shift(there, c, outs)
                        mag = w_ref[n, span] * (far - ex[n, span] if ends == "both" else far)
                        return mag, v_ref[n, span] * q_moved[c + REACH, span, rows, :]

                    def add(total, value):
                        return value if total is None else total + value

                    length = mix(o, *[math.sqrt(a * a + b * b) for a in (low, high)])
                    mag, flow = one(b)
                    if b:
                        mag2, flow2 = one(-b)
                        side_sum = add(side_sum, mag - mag2)
                        mag = mag + mag2
                    if o:
                        row_sums[o] = add(row_sums.get(o), mag)
                    if ends == "near":
                        gain = gain + length * mag
                        continue
                    gain = gain - length * mag + flow
                    if b:
                        gain = gain + flow2
                if side_sum is not None:
                    force_y = force_y - float(b) * side_sum if ends == "near" else force_y + float(b) * side_sum
            for o, low, high in chosen:
                if o:
                    part = mix(o, low, high) * row_sums[o]
                    force_x = force_x - part if ends == "near" else force_x + part
        return force_x, force_y, gain

    def duplicate_rim(x, planes):
        for plane in planes:
            x[plane, RIM, ROWS : 2 * ROWS, :] = x[plane, RIM, 0:ROWS, :]

    def finish(x, sums, drain, velocity, outs=ALL):
        span = slice(outs[0], outs[-1] + 1)
        force_x, force_y, gain = sums
        u0, u1, p = (x[plane, span, 0:ROWS, :] for plane in range(3))
        density, storage = still[0, span], still[1, span]
        v0 = velocity[0] + 0.1 * (density * force_x - 0.5 * velocity[0])
        v1 = velocity[1] + 0.1 * (density * force_y - 0.5 * velocity[1])
        pressure = p + 0.1 * storage * 0.1 * (gain - drain * p)
        return u0 + 0.1 * v0, u1 + 0.1 * v1, pressure, v0, v1

    zero = jnp.zeros((blocks, ROWS, LANES), f32)

    arrive(kinds_rim)
    duplicate_rim(own1, (3,))
    drain = weigh(True, own1)
    arrive(fields_rim)
    duplicate_rim(own1, (0, 1, 2))
    centre(own1)
    sums = evaluate(True, own1, (zero,) * 3)
    local[5].wait()
    velocity = [jnp.stack(cut(vel_v[i])) for i in range(2)]

    arrive(kinds_far)
    drain = drain + weigh(False, far1)
    arrive(fields_far)
    moving, after = [], []
    for outs in (OUTER, INNER):
        span = slice(outs[0], outs[-1] + 1)
        part = evaluate(False, far1, tuple(t[span] for t in sums), outs, outs != OUTER)
        new = finish(own1, part, drain[span], [t[span] for t in velocity], outs)
        for plane in range(3):
            own2[plane, span, 0:ROWS, :] = new[plane]
            own2[plane, span, ROWS : 2 * ROWS, :] = new[plane]
        after.append(new[3:])
        moving += send(own2, far2, fields, STRAIGHT, pl.ds(outs[0], len(outs)))
        if outs == OUTER:
            moving += send(own2, far2, fields, CORNERS)
            rim2 = send(own2, far2, fields, ACROSS)
    velocity = [jnp.concatenate(pair, axis=0) for pair in zip(*after)]

    arrive(rim2)
    duplicate_rim(own2, (0, 1, 2))
    centre(own2)
    sums = evaluate(True, own2, (zero,) * 3)
    sums = evaluate(False, None, sums, ends="near")
    finish_sends(len(messages) - 7)
    arrive(moving)
    sums = evaluate(False, far2, sums, ends="far")
    n0, n1, np_, v0, v1 = finish(own2, sums, drain, velocity)

    for k, j in enumerate(PLACES):
        at = slice(j * LANES, (j + 1) * LANES)
        out_disp[0, :, at] = n0[k]
        out_disp[1, :, at] = n1[k]
        out_vel[0, :, at] = v0[k]
        out_vel[1, :, at] = v1[k]
        out_pres[:, at] = np_[k]

    finish_sends(len(messages))


def hand_over(a, b, c, out_a, out_b, out_c, sems):
    copies = [
        pltpu.make_async_copy(source, target, sems.at[i])
        for i, (source, target) in enumerate(((a, out_a), (b, out_b), (c, out_c)))
    ]
    for copy in copies:
        copy.start()
    for copy in copies:
        copy.wait()


def body(gx_count, displacement, velocity, pressure, broken_bits, material_class, table):
    height, breadth = pressure.shape
    assert height == ROWS and breadth % LANES == 0 and breadth == len(PLACES) * LANES
    blocks = breadth // LANES
    vmem = pl.BlockSpec(memory_space=pltpu.VMEM)
    anywhere = pl.BlockSpec(memory_space=pltpu.HBM)
    f, i32 = jnp.float32, jnp.int32
    dma = pltpu.SemaphoreType.DMA
    n_own, n_far = (len(SLOTS[own]) for own in (True, False))

    def planes(n, blocks, rows):
        return pltpu.VMEM((n, blocks, rows, LANES), f)

    shapes = (displacement.shape, velocity.shape, pressure.shape)
    results = pl.pallas_call(
        functools.partial(kernel, gx_count),
        out_shape=tuple(pltpu.VMEM(s, f) for s in shapes),
        in_specs=[anywhere] * 6,
        out_specs=(vmem, vmem, vmem),
        scratch_shapes=[
            pltpu.VMEM(displacement.shape, f),
            pltpu.VMEM(velocity.shape, f),
            pltpu.VMEM(pressure.shape, f),
            pltpu.VMEM(broken_bits.shape, i32),
            pltpu.VMEM(material_class.shape, i32),
            pltpu.SMEM(table.shape, f),
            planes(4, blocks + 1, 2 * ROWS),
            planes(4, blocks + 1, 2 * ROWS),
            planes(3, blocks + 1, 2 * ROWS),
            planes(3, blocks + 1, 2 * ROWS),
            planes(SPAN, blocks + 1, 2 * ROWS),
            planes(SPAN, blocks + 1, 2 * ROWS),
            planes(SPAN, blocks, 2 * ROWS),
            planes(SPAN, blocks, 2 * ROWS),
            pltpu.VMEM((2, SPAN, blocks, 2 * ROWS, LANES), f),
            pltpu.VMEM((2, SPAN, blocks, 2 * ROWS, LANES), f),
            planes(2, table.shape[0], ROWS),
            planes(2, blocks, ROWS),
            planes(n_own, blocks, ROWS),
            planes(n_own, blocks, ROWS),
            planes(n_far, blocks, ROWS),
            planes(n_far, blocks, ROWS),
            planes(n_own, blocks, ROWS),
            planes(n_far, blocks, ROWS),
            planes(ROWS - 1, blocks + 1, ROWS),
            planes(ROWS - 1, blocks + 1, ROWS),
            planes(SPAN, blocks, ROWS),
            planes(2, blocks, ROWS),
            dma((6,)), dma((MESSAGES,)), dma((MESSAGES,)),
        ],
        compiler_params=pltpu.CompilerParams(
            collective_id=0, has_side_effects=True, vmem_limit_bytes=62 * 1024 * 1024
        ),
        name="peridynamics",
    )(displacement, velocity, pressure, broken_bits, material_class, table)
    return pl.pallas_call(
        hand_over,
        out_shape=tuple(jax.ShapeDtypeStruct(s, f) for s in shapes),
        in_specs=[vmem] * 3,
        out_specs=(anywhere,) * 3,
        scratch_shapes=[dma((3,))],
        name="hand_over",
    )(*[pltpu.with_memory_space_constraint(r, pltpu.VMEM) for r in results])


def solution(mesh):
    plane = P(("sample", "gx"), "gy")
    stack = P(None, ("sample", "gx"), "gy")
    assert mesh.shape["gy"] == 2
    return jax.shard_map(
        functools.partial(body, mesh.shape["gx"]),
        mesh=mesh,
        in_specs=(stack, stack, plane, stack, plane, P("sample", None)),
        out_specs=(stack, stack, plane),
        check_vma=False,
    )
```

```python
import functools
import math

import jax
import jax.numpy as jnp
from jax import lax
from jax.experimental import pallas as pl
from jax.experimental.pallas import tpu as pltpu
from jax.sharding import PartitionSpec as P

REACH = 6
SPAN = 2 * REACH + 1
MESH = pl.DeviceIdType.MESH
LANES = 128
ROWS = 8
OUTSIDE = -1
PLACES = (0, 3, 1, 2)
RIM = len(PLACES)
AFTER, BEFORE = (2, RIM, 3, 1), (RIM, 3, 0, 2)
OUTER, INNER, ALL = (0, 1), (2, 3), (0, 1, 2, 3)
MESSAGES = 14
STRIP = 16
HALF = 4
FAR = 3.0e38

half_width = {a: math.isqrt(37 - a * a) for a in range(-REACH, REACH + 1)}
first_bond = {}
_count = 0
for _a in range(-REACH, REACH + 1):
    first_bond[_a] = _count
    _count += 2 * half_width[_a] + 1 - (1 if _a == 0 else 0)


def bond(a, b):
    if abs(a) > REACH or abs(b) > half_width[a] or (a == 0 and b == 0):
        return None
    return first_bond[a] + b + half_width[a] - (1 if a == 0 and b > 0 else 0)


def groups_of(own):
    out = [(0, 0, 0)] if own else []
    for o in range(1, ROWS):
        out.append((o, o, o - ROWS) if own else (o, o - ROWS, o))
    return out


def columns_of(low, high):
    return max(half_width.get(low, -1), half_width.get(high, -1))


def slots_of(own):
    slots = {}
    for o, low, high in groups_of(own):
        for b in range(-columns_of(low, high), columns_of(low, high) + 1):
            if (o, b) != (0, 0):
                slots[o, b] = len(slots)
    return slots


SLOTS = {own: slots_of(own) for own in (True, False)}


def kernel(
    gx_count, disp, vel, pres, bits, klass, table,
    out_disp, out_vel, out_pres,
    disp_v, vel_v, pres_v, bits_v, klass_v, table_s,
    own1, far1, own2, far2, own_pack, far_pack,
    z_own, z_far, q_own, q_far, inv_own, inv_far, inverse, here_inv,
    w_own, v_own, w_far, v_far, ex_own, ex_far, y_own, y_far, side_b, still,
    local_sem, send_sem, recv_sem,
):
    f32 = jnp.float32
    sample, gx, gy = lax.axis_index("sample"), lax.axis_index("gx"), lax.axis_index("gy")
    height, breadth = pres.shape
    blocks = breadth // LANES
    has_up, has_down = gx > 0, gx < gx_count - 1
    up, down, mate = gx - 1, gx + 1, 1 - gy

    local = [
        pltpu.make_async_copy(table, table_s, local_sem.at[0]),
        pltpu.make_async_copy(klass, klass_v, local_sem.at[1]),
        pltpu.make_async_copy(disp, disp_v, local_sem.at[2]),
        pltpu.make_async_copy(pres, pres_v, local_sem.at[3]),
        pltpu.make_async_copy(bits, bits_v, local_sem.at[4]),
        pltpu.make_async_copy(vel, vel_v, local_sem.at[5]),
    ]
    for copy in local:
        copy.start()

    for plane in range(4):
        fill = float(OUTSIDE) if plane == 3 else 0.0
        far1[plane] = jnp.full(far1.shape[1:], fill, f32)
        if plane < 3:
            far2[plane] = jnp.zeros(far2.shape[1:], f32)
    far_pack[...] = jnp.full(far_pack.shape, float(OUTSIDE), f32)

    barrier = pltpu.get_barrier_semaphore()

    def greet(x, y):
        pl.semaphore_signal(barrier, inc=1, device_id=(sample, x, y), device_id_type=MESH)

    @pl.when(has_up)
    def _():
        greet(up, gy)
        greet(up, mate)

    @pl.when(has_down)
    def _():
        greet(down, gy)
        greet(down, mate)

    greet(gx, mate)

    def cut(value):
        return [value[:, j * LANES : (j + 1) * LANES] for j in PLACES]

    def put(target, plane, value):
        for j, piece in enumerate(cut(value)):
            for rows in (slice(0, ROWS), slice(ROWS, 2 * ROWS)):
                target[plane, j, rows, :] = piece

    for i in (1, 2, 3):
        local[i].wait()
    put(own1, 3, klass_v[...].astype(f32))
    put(own1, 0, disp_v[0])
    put(own1, 1, disp_v[1])
    put(own1, 2, pres_v[...])

    edge, rim = pl.ds(1 - gy, 1), pl.ds(RIM, 1)
    to_up = (pl.ds(0, REACH), pl.ds(ROWS, REACH))
    to_down = (pl.ds(ROWS - REACH, REACH), pl.ds(ROWS - REACH, REACH))
    routes = (
        (has_up, has_down, (sample, up, gy), to_up),
        (has_down, has_up, (sample, down, gy), to_down),
        (has_up, has_down, (sample, up, mate), to_up),
        (has_down, has_up, (sample, down, mate), to_down),
        (None, None, (sample, gx, mate), None),
    )
    STRAIGHT, CORNERS, ACROSS = (0, 1), (2, 3), (4,)
    messages = []

    def when(condition, act):
        if condition is None:
            act()
        else:
            pl.when(condition)(act)

    sublane = lax.broadcasted_iota(jnp.int32, (ROWS, LANES), 0)
    lane = lax.broadcasted_iota(jnp.int32, (ROWS, LANES), 1)

    def pack(x, planes, which):
        strip = ((lane - (1 - gy) * (LANES - STRIP)) & (LANES - 1)) >> 4
        total = None
        for plane in range(planes):
            value = x[plane, pl.ds(1 - gy, 1), 0:ROWS, :][0]
            if plane:
                total = jnp.where(strip == plane, pltpu.roll(value, STRIP * plane, 1), total)
            else:
                total = value
        own_pack[which] = total

    def unpack(x, planes, which):
        for rows in (slice(0, ROWS), slice(ROWS, 2 * ROWS)):
            value = far_pack[which, rows, :]
            for plane in range(planes):
                x[plane, RIM, rows, :] = (
                    pltpu.roll(value, LANES - STRIP * plane, 1) if plane else value
                )

    def send(routes_used, source, target):
        sent = []
        for n in routes_used:
            going, coming, device, rows = routes[n]
            here, there = (pl.ds(0, ROWS),) * 2 if rows is None else rows
            m = len(messages)
            copy = pltpu.make_async_remote_copy(
                src_ref=source(here), dst_ref=target(there),
                send_sem=send_sem.at[m], recv_sem=recv_sem.at[m],
                device_id=device, device_id_type=MESH,
            )
            when(going, copy.start)
            messages.append((going, copy))
            sent.append((coming, copy))
        return sent

    def send_straight(own, far, planes, blocks):
        return send(
            STRAIGHT, lambda r: own.at[planes, blocks, r], lambda r: far.at[planes, blocks, r]
        )

    def send_across(own):
        return send(ACROSS, lambda r: own.at[:, edge, r], lambda r: own.at[:, rim, r])

    def send_corners(which):
        return send(CORNERS, lambda r: own_pack.at[which, r], lambda r: far_pack.at[which, r])

    waited = []

    def finish_sends(count):
        for going, copy in messages[len(waited) : count]:
            when(going, copy.wait_send)
            waited.append(copy)

    def arrive(sent):
        for coming, copy in sent:
            when(coming, copy.wait_recv)

    pack(own1, 4, 0)
    pl.semaphore_wait(
        barrier, 1 + 2 * has_up.astype(jnp.int32) + 2 * has_down.astype(jnp.int32)
    )
    fields, kinds = pl.ds(0, 3), pl.ds(3, 1)
    four = pl.ds(0, blocks)
    four = pl.ds(0, blocks)
    kinds_far = send_straight(own1, far1, kinds, four) + send_corners(0)
    fields_far = send_straight(own1, far1, fields, four)
    rim1 = send_across(own1)

    def mix(o, low, high, kind=f32):
        return kind(low) if low == high else jnp.where(sublane < ROWS - o, kind(low), kind(high))

    local[0].wait()

    def look_up(which, member):
        value = jnp.full(which.shape, table_s[table.shape[0] - 1, member], f32)
        for c in range(table.shape[0] - 1):
            value = jnp.where(which == c, table_s[c, member], value)
        return value

    classes = table.shape[0]
    for m in range(2):
        for c in range(classes):
            inverse[m, c] = 1.0 / jnp.full((ROWS, LANES), table_s[c, m], f32)

    def inverses(which):
        out = [jnp.full(which.shape, FAR, f32)] * 2
        for c in range(classes):
            chosen = which == float(c)
            out = [jnp.where(chosen, inverse[m, c], out[m]) for m in range(2)]
        return out

    for m, value in enumerate(inverses(own1[3, :blocks, 0:ROWS, :])):
        here_inv[m] = value

    klass_own = klass_v[...]
    for plane, member in ((0, 2), (1, 3)):
        for j, piece in enumerate(cut(look_up(klass_own, member))):
            still[plane, j] = piece
    local[4].wait()
    for j in range(blocks):
        words = [bits_v[w, :, PLACES[j] * LANES : (PLACES[j] + 1) * LANES] for w in range(bits.shape[0])]

        def broken(a, b):
            k = bond(a, b)
            return jnp.int32(1) if k is None else words[k // 12] & (1 << (k % 12))

        for own, w_to, v_to in ((True, w_own, v_own), (False, w_far, v_far)):
            for o, low, high in groups_of(own):
                for b in range(-columns_of(low, high), columns_of(low, high) + 1):
                    if (o, b) not in SLOTS[own]:
                        continue
                    n = SLOTS[own][o, b]
                    one = broken(low, b)
                    if o:
                        one = jnp.where(sublane < ROWS - o, one, broken(high, b))
                    squares = [a * a + b * b for a in (low, high)]
                    w_to[n, j] = jnp.where(one == 0, mix(o, *[2.0 / x**2 for x in squares]), 0.0)
                    v_to[n, j] = jnp.where(one == 0, mix(o, *[2.0 / x for x in squares]), 0.0)

    def load(get, which):
        runs = []
        for k in which:
            if runs and runs[-1][1] == k:
                runs[-1][1] = k + 1
            else:
                runs.append([k, k + 1])
        pieces = [get(*run) for run in runs]
        return pieces[0] if len(pieces) == 1 else jnp.concatenate(pieces, axis=0)

    def shift(get, b, outs=ALL):
        if b == 0:
            return load(get, outs)
        other = [(AFTER if b > 0 else BEFORE)[k] for k in outs]
        sources = sorted(set(outs) | set(other))
        turned = pltpu.roll(load(get, sources), (-b) % LANES, 2)

        def take(which):
            at = [sources.index(k) for k in which]
            return load(lambda i, j: turned[i:j], at)

        return jnp.where(lane < LANES - b if b > 0 else lane >= -b, take(outs), take(other))

    def tiles(own):
        top, bottom = slice(0, ROWS), slice(ROWS, 2 * ROWS)
        return [(top, (top, bottom))] if own else [(top, (top,)), (bottom, (bottom,))]

    valid = (lane < LANES // 2) == (gy == 0)

    def weigh(own, x):
        w_ref, v_ref, inv = (w_own, v_own, inv_own) if own else (w_far, v_far, inv_far)
        known = []
        for read, write in tiles(own):
            value = x[3, :, read, :]
            rim_value = jnp.where(valid, value[blocks:], float(OUTSIDE))
            known.append(inverses(jnp.concatenate([value[:blocks], rim_value], axis=0)))
        drain = jnp.zeros((blocks, ROWS, LANES), f32)
        for b in sorted(range(-REACH, REACH + 1), key=abs):
            for (read, write), pair in zip(tiles(own), known):
                for m, value in enumerate(pair):
                    moved = shift(lambda i, j: value[i:j], b)
                    for rows in write:
                        inv[m, b + REACH, :, rows, :] = moved
            for o, low, high in groups_of(own):
                if (o, b) not in SLOTS[own]:
                    continue
                n = SLOTS[own][o, b]
                cubes = [0.25 * math.sqrt(a * a + b * b) ** 3 for a in (low, high)]
                weight, flow = (
                    ref[n]
                    * pl.reciprocal(
                        here_inv[m] + inv[m, b + REACH, :, pl.ds(o, ROWS), :], approx=True
                    )
                    for m, ref in enumerate((w_ref, v_ref))
                )
                share = mix(o, *cubes) * weight
                w_ref[n] = weight
                v_ref[n] = flow - share
                drain = drain + (flow + share)
        return drain

    def centre(x):
        u, v, p = (x[plane, :blocks, 0:ROWS, :] for plane in range(3))
        for b in range(-REACH, REACH + 1):
            side_b[b + REACH] = float(b) * v + (0.25 * b * b) * p
        for own, target in ((True, ex_own), (False, ex_far)):
            for o, low, high in groups_of(own):
                here = mix(o, low, high) * u + mix(o, 0.25 * low * low, 0.25 * high * high) * p
                for b in range(-columns_of(low, high), columns_of(low, high) + 1):
                    if (o, b) in SLOTS[own]:
                        target[SLOTS[own][o, b]] = here if b == 0 else here + side_b[b + REACH]

    def evaluate(own, x, sums, outs=ALL, ready=False, ends="both"):
        w_ref, v_ref, ex, z, q_moved, y = (
            (w_own, v_own, ex_own, z_own, q_own, y_own)
            if own
            else (w_far, v_far, ex_far, z_far, q_far, y_far)
        )
        slots = SLOTS[own]
        force_x, force_y, gain = sums
        span = slice(outs[0], outs[-1] + 1)
        ready = ready or ends == "near"
        if not ready:
            for o, low, high in groups_of(own):
                if o:
                    rows = pl.ds(o, ROWS)
                    y[o - 1] = (
                        mix(o, low, high) * x[0, :, rows, :]
                        - mix(o, 0.25 * low * low, 0.25 * high * high) * x[2, :, rows, :]
                    )
        groups = groups_of(own)
        sets = (groups,) if len(outs) < len(ALL) else (groups[: HALF], groups[HALF:])
        for chosen in sets:
            row_sums = {}
            for b in range(REACH + 1):
                if not ready and chosen is sets[0]:
                    for read, write in tiles(own):
                        if b:
                            v, q = x[1, :, read, :], x[2, :, read, :]
                            bv, bq = float(b) * v, (-0.25 * b * b) * q
                            for rows in write:
                                z[REACH + b, :, rows, :] = bq + bv
                                z[REACH - b, :, rows, :] = bq - bv
                        for c in (b, -b) if b else (0,):
                            moved = shift(lambda i, j: x[2, i:j, read, :], c)
                            for rows in write:
                                q_moved[c + REACH, :, rows, :] = moved
                side_sum = None
                for o, low, high in chosen:
                    if (o, b) not in slots:
                        continue
                    rows = pl.ds(o, ROWS)

                    def one(c):
                        n = slots[o, c]

                        def there(i, j):
                            if c == 0:
                                return y[o - 1, i:j]
                            side = z[c + REACH, i:j, rows, :]
                            return side + y[o - 1, i:j] if o else side

                        if ends == "near":
                            return w_ref[n, span] * ex[n, span], None
                        far = shift(there, c, outs)
                        mag = w_ref[n, span] * (far - ex[n, span] if ends == "both" else far)
                        return mag, v_ref[n, span] * q_moved[c + REACH, span, rows, :]

                    def add(total, value):
                        return value if total is None else total + value

                    length = mix(o, *[math.sqrt(a * a + b * b) for a in (low, high)])
                    mag, flow = one(b)
                    if b:
                        mag2, flow2 = one(-b)
                        side_sum = add(side_sum, mag - mag2)
                        mag = mag + mag2
                    if o:
                        row_sums[o] = add(row_sums.get(o), mag)
                    if ends == "near":
                        gain = gain + length * mag
                        continue
                    gain = gain - length * mag + flow
                    if b:
                        gain = gain + flow2
                if side_sum is not None:
                    force_y = force_y - float(b) * side_sum if ends == "near" else force_y + float(b) * side_sum
            for o, low, high in chosen:
                if o:
                    part = mix(o, low, high) * row_sums[o]
                    force_x = force_x - part if ends == "near" else force_x + part
        return force_x, force_y, gain

    def duplicate_rim(x, planes):
        for plane in planes:
            x[plane, RIM, ROWS : 2 * ROWS, :] = x[plane, RIM, 0:ROWS, :]

    def finish(x, sums, drain, velocity, outs=ALL):
        span = slice(outs[0], outs[-1] + 1)
        force_x, force_y, gain = sums
        u0, u1, p = (x[plane, span, 0:ROWS, :] for plane in range(3))
        density, storage = still[0, span], still[1, span]
        v0 = velocity[0] + 0.1 * (density * force_x - 0.5 * velocity[0])
        v1 = velocity[1] + 0.1 * (density * force_y - 0.5 * velocity[1])
        pressure = p + 0.1 * storage * 0.1 * (gain - drain * p)
        return u0 + 0.1 * v0, u1 + 0.1 * v1, pressure, v0, v1

    zero = jnp.zeros((blocks, ROWS, LANES), f32)

    arrive(rim1)
    duplicate_rim(own1, range(4))
    drain = weigh(True, own1)
    centre(own1)
    sums = evaluate(True, own1, (zero,) * 3)
    local[5].wait()
    velocity = [jnp.stack(cut(vel_v[i])) for i in range(2)]

    arrive(kinds_far)
    unpack(far1, 4, 0)
    drain = drain + weigh(False, far1)
    arrive(fields_far)
    moving, after = [], []
    for outs in (OUTER, INNER):
        span = slice(outs[0], outs[-1] + 1)
        part = evaluate(False, far1, tuple(t[span] for t in sums), outs, outs != OUTER)
        new = finish(own1, part, drain[span], [t[span] for t in velocity], outs)
        for plane in range(3):
            own2[plane, span, 0:ROWS, :] = new[plane]
            own2[plane, span, ROWS : 2 * ROWS, :] = new[plane]
        after.append(new[3:])
        moving += send_straight(own2, far2, fields, pl.ds(outs[0], len(outs)))
        if outs == OUTER:
            pack(own2, 3, 1)
            moving += send_corners(1)
            rim2 = send_across(own2)
    velocity = [jnp.concatenate(pair, axis=0) for pair in zip(*after)]

    arrive(rim2)
    duplicate_rim(own2, range(3))
    centre(own2)
    sums = evaluate(True, own2, (zero,) * 3)
    sums = evaluate(False, None, sums, ends="near")
    finish_sends(len(messages) - 7)
    arrive(moving)
    unpack(far2, 3, 1)
    sums = evaluate(False, far2, sums, ends="far")
    n0, n1, np_, v0, v1 = finish(own2, sums, drain, velocity)

    for k, j in enumerate(PLACES):
        at = slice(j * LANES, (j + 1) * LANES)
        out_disp[0, :, at] = n0[k]
        out_disp[1, :, at] = n1[k]
        out_vel[0, :, at] = v0[k]
        out_vel[1, :, at] = v1[k]
        out_pres[:, at] = np_[k]

    finish_sends(len(messages))


def hand_over(a, b, c, out_a, out_b, out_c, sems):
    copies = [
        pltpu.make_async_copy(source, target, sems.at[i])
        for i, (source, target) in enumerate(((a, out_a), (b, out_b), (c, out_c)))
    ]
    for copy in copies:
        copy.start()
    for copy in copies:
        copy.wait()


def body(gx_count, displacement, velocity, pressure, broken_bits, material_class, table):
    height, breadth = pressure.shape
    assert height == ROWS and breadth % LANES == 0 and breadth == len(PLACES) * LANES
    blocks = breadth // LANES
    vmem = pl.BlockSpec(memory_space=pltpu.VMEM)
    anywhere = pl.BlockSpec(memory_space=pltpu.HBM)
    f, i32 = jnp.float32, jnp.int32
    dma = pltpu.SemaphoreType.DMA
    n_own, n_far = (len(SLOTS[own]) for own in (True, False))

    def planes(n, blocks, rows):
        return pltpu.VMEM((n, blocks, rows, LANES), f)

    shapes = (displacement.shape, velocity.shape, pressure.shape)
    results = pl.pallas_call(
        functools.partial(kernel, gx_count),
        out_shape=tuple(pltpu.VMEM(s, f) for s in shapes),
        in_specs=[anywhere] * 6,
        out_specs=(vmem, vmem, vmem),
        scratch_shapes=[
            pltpu.VMEM(displacement.shape, f),
            pltpu.VMEM(velocity.shape, f),
            pltpu.VMEM(pressure.shape, f),
            pltpu.VMEM(broken_bits.shape, i32),
            pltpu.VMEM(material_class.shape, i32),
            pltpu.SMEM(table.shape, f),
            planes(4, blocks + 1, 2 * ROWS),
            planes(4, blocks + 1, 2 * ROWS),
            planes(3, blocks + 1, 2 * ROWS),
            planes(3, blocks + 1, 2 * ROWS),
            pltpu.VMEM((2, ROWS, LANES), f),
            pltpu.VMEM((2, 2 * ROWS, LANES), f),
            planes(SPAN, blocks + 1, 2 * ROWS),
            planes(SPAN, blocks + 1, 2 * ROWS),
            planes(SPAN, blocks, 2 * ROWS),
            planes(SPAN, blocks, 2 * ROWS),
            pltpu.VMEM((2, SPAN, blocks, 2 * ROWS, LANES), f),
            pltpu.VMEM((2, SPAN, blocks, 2 * ROWS, LANES), f),
            planes(2, table.shape[0], ROWS),
            planes(2, blocks, ROWS),
            planes(n_own, blocks, ROWS),
            planes(n_own, blocks, ROWS),
            planes(n_far, blocks, ROWS),
            planes(n_far, blocks, ROWS),
            planes(n_own, blocks, ROWS),
            planes(n_far, blocks, ROWS),
            planes(ROWS - 1, blocks + 1, ROWS),
            planes(ROWS - 1, blocks + 1, ROWS),
            planes(SPAN, blocks, ROWS),
            planes(2, blocks, ROWS),
            dma((6,)), dma((MESSAGES,)), dma((MESSAGES,)),
        ],
        compiler_params=pltpu.CompilerParams(
            collective_id=0, has_side_effects=True, vmem_limit_bytes=62 * 1024 * 1024
        ),
        name="peridynamics",
    )(displacement, velocity, pressure, broken_bits, material_class, table)
    return pl.pallas_call(
        hand_over,
        out_shape=tuple(jax.ShapeDtypeStruct(s, f) for s in shapes),
        in_specs=[vmem] * 3,
        out_specs=(anywhere,) * 3,
        scratch_shapes=[dma((3,))],
        name="hand_over",
    )(*[pltpu.with_memory_space_constraint(r, pltpu.VMEM) for r in results])


def solution(mesh):
    plane = P(("sample", "gx"), "gy")
    stack = P(None, ("sample", "gx"), "gy")
    assert mesh.shape["gy"] == 2
    return jax.shard_map(
        functools.partial(body, mesh.shape["gx"]),
        mesh=mesh,
        in_specs=(stack, stack, plane, stack, plane, P("sample", None)),
        out_specs=(stack, stack, plane),
        check_vma=False,
    )
```

```python
import functools
import math

import jax
import jax.numpy as jnp
from jax import lax
from jax.experimental import pallas as pl
from jax.experimental.pallas import tpu as pltpu
from jax.sharding import PartitionSpec as P

REACH = 6
SPAN = 2 * REACH + 1
MESH = pl.DeviceIdType.MESH
LANES = 128
ROWS = 8
OUTSIDE = -1
PLACES = (0, 3, 1, 2)
RIM = len(PLACES)
AFTER, BEFORE = (2, RIM, 3, 1), (RIM, 3, 0, 2)
OUTER, INNER, ALL = (0, 1), (2, 3), (0, 1, 2, 3)
MESSAGES = 14
STRIP = 16
HALF = 4
JOINED = (1, 2, 3)
Y_SLOTS = ROWS + len(JOINED)
FAR = 3.0e38

half_width = {a: math.isqrt(37 - a * a) for a in range(-REACH, REACH + 1)}
first_bond = {}
_count = 0
for _a in range(-REACH, REACH + 1):
    first_bond[_a] = _count
    _count += 2 * half_width[_a] + 1 - (1 if _a == 0 else 0)


def bond(a, b):
    if abs(a) > REACH or abs(b) > half_width[a] or (a == 0 and b == 0):
        return None
    return first_bond[a] + b + half_width[a] - (1 if a == 0 and b > 0 else 0)


def groups_of(own):
    offsets = range(ROWS) if own else range(2, ROWS - 1)
    out = [(o, o, o - ROWS if o else 0) if own else (o, o - ROWS, o) for o in offsets]
    return out if own else out + [(-m, -m, m) for m in JOINED]


def columns_of(low, high):
    return max(half_width.get(low, -1), half_width.get(high, -1))


def slots_of(own):
    slots = {}
    for o, low, high in groups_of(own):
        widths = half_width.get(low, -1), half_width.get(high, -1)
        for b in range(-max(widths), max(widths) + 1):
            one_sided = abs(b) > min(widths)
            if not own and o > 0 and one_sided:
                continue
            if o < 0 and abs(b) <= half_width.get(ROWS + o, -1):
                continue
            if low or b:
                slots[o, b] = len(slots)
    return slots


SLOTS = {own: slots_of(own) for own in (True, False)}


def kernel(
    gx_count, disp, vel, pres, bits, klass, table,
    out_disp, out_vel, out_pres,
    disp_v, vel_v, pres_v, bits_v, klass_v, table_s,
    own1, far1, own2, far2, own_pack, far_pack,
    z_own, z_far, q_own, q_far, inv_own, inv_far, inverse, here_inv,
    w_own, v_own, w_far, v_far, ex_own, ex_far, y_own, y_far, side_b, still,
    local_sem, send_sem, recv_sem,
):
    f32 = jnp.float32
    sample, gx, gy = lax.axis_index("sample"), lax.axis_index("gx"), lax.axis_index("gy")
    height, breadth = pres.shape
    blocks = breadth // LANES
    has_up, has_down = gx > 0, gx < gx_count - 1
    up, down, mate = gx - 1, gx + 1, 1 - gy

    local = [
        pltpu.make_async_copy(table, table_s, local_sem.at[0]),
        pltpu.make_async_copy(klass, klass_v, local_sem.at[1]),
        pltpu.make_async_copy(disp, disp_v, local_sem.at[2]),
        pltpu.make_async_copy(pres, pres_v, local_sem.at[3]),
        pltpu.make_async_copy(bits, bits_v, local_sem.at[4]),
        pltpu.make_async_copy(vel, vel_v, local_sem.at[5]),
    ]
    for copy in local:
        copy.start()

    for plane in range(4):
        fill = float(OUTSIDE) if plane == 3 else 0.0
        far1[plane] = jnp.full(far1.shape[1:], fill, f32)
        if plane < 3:
            far2[plane] = jnp.zeros(far2.shape[1:], f32)
    far_pack[...] = jnp.full(far_pack.shape, float(OUTSIDE), f32)

    barrier = pltpu.get_barrier_semaphore()

    def greet(x, y):
        pl.semaphore_signal(barrier, inc=1, device_id=(sample, x, y), device_id_type=MESH)

    @pl.when(has_up)
    def _():
        greet(up, gy)
        greet(up, mate)

    @pl.when(has_down)
    def _():
        greet(down, gy)
        greet(down, mate)

    greet(gx, mate)

    def cut(value):
        return [value[:, j * LANES : (j + 1) * LANES] for j in PLACES]

    def put(target, plane, value):
        for j, piece in enumerate(cut(value)):
            for rows in (slice(0, ROWS), slice(ROWS, 2 * ROWS)):
                target[plane, j, rows, :] = piece

    for i in (1, 2, 3):
        local[i].wait()
    put(own1, 3, klass_v[...].astype(f32))
    put(own1, 0, disp_v[0])
    put(own1, 1, disp_v[1])
    put(own1, 2, pres_v[...])

    edge, rim = pl.ds(1 - gy, 1), pl.ds(RIM, 1)
    to_up = (pl.ds(0, REACH), pl.ds(ROWS, REACH))
    to_down = (pl.ds(ROWS - REACH, REACH), pl.ds(ROWS - REACH, REACH))
    routes = (
        (has_up, has_down, (sample, up, gy), to_up),
        (has_down, has_up, (sample, down, gy), to_down),
        (has_up, has_down, (sample, up, mate), to_up),
        (has_down, has_up, (sample, down, mate), to_down),
        (None, None, (sample, gx, mate), None),
    )
    STRAIGHT, CORNERS, ACROSS = (0, 1), (2, 3), (4,)
    messages = []

    def when(condition, act):
        if condition is None:
            act()
        else:
            pl.when(condition)(act)

    sublane = lax.broadcasted_iota(jnp.int32, (ROWS, LANES), 0)
    lane = lax.broadcasted_iota(jnp.int32, (ROWS, LANES), 1)

    def pack(x, planes, which):
        strip = ((lane - (1 - gy) * (LANES - STRIP)) & (LANES - 1)) >> 4
        total = None
        for plane in range(planes):
            value = x[plane, pl.ds(1 - gy, 1), 0:ROWS, :][0]
            if plane:
                total = jnp.where(strip == plane, pltpu.roll(value, STRIP * plane, 1), total)
            else:
                total = value
        own_pack[which] = total

    def unpack(x, planes, which):
        for rows in (slice(0, ROWS), slice(ROWS, 2 * ROWS)):
            value = far_pack[which, rows, :]
            for plane in range(planes):
                x[plane, RIM, rows, :] = (
                    pltpu.roll(value, LANES - STRIP * plane, 1) if plane else value
                )

    def send(routes_used, source, target):
        sent = []
        for n in routes_used:
            going, coming, device, rows = routes[n]
            here, there = (pl.ds(0, ROWS),) * 2 if rows is None else rows
            m = len(messages)
            copy = pltpu.make_async_remote_copy(
                src_ref=source(here), dst_ref=target(there),
                send_sem=send_sem.at[m], recv_sem=recv_sem.at[m],
                device_id=device, device_id_type=MESH,
            )
            when(going, copy.start)
            messages.append((going, copy))
            sent.append((coming, copy))
        return sent

    def send_straight(own, far, planes, blocks):
        return send(
            STRAIGHT, lambda r: own.at[planes, blocks, r], lambda r: far.at[planes, blocks, r]
        )

    def send_across(own):
        return send(ACROSS, lambda r: own.at[:, edge, r], lambda r: own.at[:, rim, r])

    def send_corners(which):
        return send(CORNERS, lambda r: own_pack.at[which, r], lambda r: far_pack.at[which, r])

    waited = []

    def finish_sends(count):
        for going, copy in messages[len(waited) : count]:
            when(going, copy.wait_send)
            waited.append(copy)

    def arrive(sent):
        for coming, copy in sent:
            when(coming, copy.wait_recv)

    pack(own1, 4, 0)
    pl.semaphore_wait(
        barrier, 1 + 2 * has_up.astype(jnp.int32) + 2 * has_down.astype(jnp.int32)
    )
    fields, kinds = pl.ds(0, 3), pl.ds(3, 1)
    four = pl.ds(0, blocks)
    four = pl.ds(0, blocks)
    kinds_far = send_straight(own1, far1, kinds, four) + send_corners(0)
    fields_far = send_straight(own1, far1, fields, four)
    rim1 = send_across(own1)

    def first_rows(o):
        return sublane < (ROWS - o if o >= 0 else -o)

    def mix(o, low, high, kind=f32):
        return kind(low) if low == high else jnp.where(first_rows(o), kind(low), kind(high))

    def window(get, o):
        if o >= 0:
            return get(pl.ds(o, ROWS))
        return jnp.where(first_rows(o), get(pl.ds(ROWS + o, ROWS)), get(pl.ds(-o, ROWS)))

    local[0].wait()

    def look_up(which, member):
        value = jnp.full(which.shape, table_s[table.shape[0] - 1, member], f32)
        for c in range(table.shape[0] - 1):
            value = jnp.where(which == c, table_s[c, member], value)
        return value

    classes = table.shape[0]
    for m in range(2):
        for c in range(classes):
            inverse[m, c] = 1.0 / jnp.full((ROWS, LANES), table_s[c, m], f32)

    def inverses(which):
        out = [jnp.full(which.shape, FAR, f32)] * 2
        for c in range(classes):
            chosen = which == float(c)
            out = [jnp.where(chosen, inverse[m, c], out[m]) for m in range(2)]
        return out

    for m, value in enumerate(inverses(own1[3, :blocks, 0:ROWS, :])):
        here_inv[m] = value

    klass_own = klass_v[...]
    for plane, member in ((0, 2), (1, 3)):
        for j, piece in enumerate(cut(look_up(klass_own, member))):
            still[plane, j] = piece
    local[4].wait()
    for j in range(blocks):
        words = [bits_v[w, :, PLACES[j] * LANES : (PLACES[j] + 1) * LANES] for w in range(bits.shape[0])]

        def broken(a, b):
            k = bond(a, b)
            return jnp.int32(1) if k is None else words[k // 12] & (1 << (k % 12))

        for own, w_to, v_to in ((True, w_own, v_own), (False, w_far, v_far)):
            for o, low, high in groups_of(own):
                for b in range(-columns_of(low, high), columns_of(low, high) + 1):
                    if (o, b) not in SLOTS[own]:
                        continue
                    n = SLOTS[own][o, b]
                    one = broken(low, b)
                    if low != high:
                        one = jnp.where(first_rows(o), one, broken(high, b))
                    if o < 0:
                        one = jnp.where((sublane >= -o) & (sublane < ROWS + o), 1, one)
                    squares = [a * a + b * b for a in (low, high)]
                    w_to[n, j] = jnp.where(one == 0, mix(o, *[2.0 / x**2 for x in squares]), 0.0)
                    v_to[n, j] = jnp.where(one == 0, mix(o, *[2.0 / x for x in squares]), 0.0)

    def load(get, which):
        runs = []
        for k in which:
            if runs and runs[-1][1] == k:
                runs[-1][1] = k + 1
            else:
                runs.append([k, k + 1])
        pieces = [get(*run) for run in runs]
        return pieces[0] if len(pieces) == 1 else jnp.concatenate(pieces, axis=0)

    def shift(get, b, outs=ALL):
        if b == 0:
            return load(get, outs)
        other = [(AFTER if b > 0 else BEFORE)[k] for k in outs]
        sources = sorted(set(outs) | set(other))
        turned = pltpu.roll(load(get, sources), (-b) % LANES, 2)

        def take(which):
            at = [sources.index(k) for k in which]
            return load(lambda i, j: turned[i:j], at)

        return jnp.where(lane < LANES - b if b > 0 else lane >= -b, take(outs), take(other))

    def tiles(own):
        top, bottom = slice(0, ROWS), slice(ROWS, 2 * ROWS)
        return [(top, (top, bottom))] if own else [(top, (top,)), (bottom, (bottom,))]

    valid = (lane < LANES // 2) == (gy == 0)

    def weigh(own, x):
        w_ref, v_ref, inv = (w_own, v_own, inv_own) if own else (w_far, v_far, inv_far)
        known = []
        for read, write in tiles(own):
            value = x[3, :, read, :]
            rim_value = jnp.where(valid, value[blocks:], float(OUTSIDE))
            known.append(inverses(jnp.concatenate([value[:blocks], rim_value], axis=0)))
        drain = jnp.zeros((blocks, ROWS, LANES), f32)
        for b in sorted(range(-REACH, REACH + 1), key=abs):
            for (read, write), pair in zip(tiles(own), known):
                for m, value in enumerate(pair):
                    moved = shift(lambda i, j: value[i:j], b)
                    for rows in write:
                        inv[m, b + REACH, :, rows, :] = moved
            for o, low, high in groups_of(own):
                if (o, b) not in SLOTS[own]:
                    continue
                n = SLOTS[own][o, b]
                cubes = [0.25 * math.sqrt(a * a + b * b) ** 3 for a in (low, high)]
                weight, flow = (
                    ref[n]
                    * pl.reciprocal(
                        here_inv[m] + window(lambda r: inv[m, b + REACH, :, r, :], o),
                        approx=True,
                    )
                    for m, ref in enumerate((w_ref, v_ref))
                )
                share = mix(o, *cubes) * weight
                w_ref[n] = weight
                v_ref[n] = flow - share
                drain = drain + (flow + share)
        return drain

    def centre(x):
        u, v, p = (x[plane, :blocks, 0:ROWS, :] for plane in range(3))
        for b in range(-REACH, REACH + 1):
            side_b[b + REACH] = float(b) * v + (0.25 * b * b) * p
        for own, target in ((True, ex_own), (False, ex_far)):
            for o, low, high in groups_of(own):
                here = mix(o, low, high) * u + mix(o, 0.25 * low * low, 0.25 * high * high) * p
                for b in range(-columns_of(low, high), columns_of(low, high) + 1):
                    if (o, b) in SLOTS[own]:
                        target[SLOTS[own][o, b]] = here if b == 0 else here + side_b[b + REACH]

    def evaluate(own, x, sums, outs=ALL, ready=False, ends="both"):
        w_ref, v_ref, ex, z, q_moved, y = (
            (w_own, v_own, ex_own, z_own, q_own, y_own)
            if own
            else (w_far, v_far, ex_far, z_far, q_far, y_far)
        )
        slots = SLOTS[own]
        force_x, force_y, gain = sums
        span = slice(outs[0], outs[-1] + 1)
        ready = ready or ends == "near"
        if not ready:
            for o, low, high in groups_of(own):
                if low:
                    u, q = (window(lambda r: x[m, :, r, :], o) for m in (0, 2))
                    y[o % Y_SLOTS] = (
                        mix(o, low, high) * u
                        - mix(o, 0.25 * low * low, 0.25 * high * high) * q
                    )
        groups = groups_of(own)
        sets = (groups,) if len(outs) < len(ALL) else (groups[: HALF], groups[HALF:])
        for chosen in sets:
            row_sums = {}
            for b in range(REACH + 1):
                if not ready and chosen is sets[0]:
                    for read, write in tiles(own):
                        if b:
                            v, q = x[1, :, read, :], x[2, :, read, :]
                            bv, bq = float(b) * v, (-0.25 * b * b) * q
                            for rows in write:
                                z[REACH + b, :, rows, :] = bq + bv
                                z[REACH - b, :, rows, :] = bq - bv
                        for c in (b, -b) if b else (0,):
                            moved = shift(lambda i, j: x[2, i:j, read, :], c)
                            for rows in write:
                                q_moved[c + REACH, :, rows, :] = moved
                side_sum = None
                for o, low, high in chosen:
                    if (o, b) not in slots:
                        continue
                    def one(c):
                        n = slots[o, c]

                        def there(i, j):
                            if c == 0:
                                return y[o % Y_SLOTS, i:j]
                            side = window(lambda r: z[c + REACH, i:j, r, :], o)
                            return side + y[o % Y_SLOTS, i:j] if low else side

                        if ends == "near":
                            return w_ref[n, span] * ex[n, span], None
                        far = shift(there, c, outs)
                        mag = w_ref[n, span] * (far - ex[n, span] if ends == "both" else far)
                        moved = window(lambda r: q_moved[c + REACH, span, r, :], o)
                        return mag, v_ref[n, span] * moved

                    def add(total, value):
                        return value if total is None else total + value

                    length = mix(o, *[math.sqrt(a * a + b * b) for a in (low, high)])
                    mag, flow = one(b)
                    if b:
                        mag2, flow2 = one(-b)
                        side_sum = add(side_sum, mag - mag2)
                        mag = mag + mag2
                    if low:
                        row_sums[o] = add(row_sums.get(o), mag)
                    if ends == "near":
                        gain = gain + length * mag
                        continue
                    gain = gain - length * mag + flow
                    if b:
                        gain = gain + flow2
                if side_sum is not None:
                    force_y = force_y - float(b) * side_sum if ends == "near" else force_y + float(b) * side_sum
            for o, low, high in chosen:
                if low:
                    part = mix(o, low, high) * row_sums[o]
                    force_x = force_x - part if ends == "near" else force_x + part
        return force_x, force_y, gain

    def duplicate_rim(x, planes):
        for plane in planes:
            x[plane, RIM, ROWS : 2 * ROWS, :] = x[plane, RIM, 0:ROWS, :]

    def finish(x, sums, drain, velocity, outs=ALL):
        span = slice(outs[0], outs[-1] + 1)
        force_x, force_y, gain = sums
        u0, u1, p = (x[plane, span, 0:ROWS, :] for plane in range(3))
        density, storage = still[0, span], still[1, span]
        v0 = velocity[0] + 0.1 * (density * force_x - 0.5 * velocity[0])
        v1 = velocity[1] + 0.1 * (density * force_y - 0.5 * velocity[1])
        pressure = p + 0.1 * storage * 0.1 * (gain - drain * p)
        return u0 + 0.1 * v0, u1 + 0.1 * v1, pressure, v0, v1

    zero = jnp.zeros((blocks, ROWS, LANES), f32)

    arrive(rim1)
    duplicate_rim(own1, range(4))
    drain = weigh(True, own1)
    centre(own1)
    sums = evaluate(True, own1, (zero,) * 3)
    local[5].wait()
    velocity = [jnp.stack(cut(vel_v[i])) for i in range(2)]

    arrive(kinds_far)
    unpack(far1, 4, 0)
    drain = drain + weigh(False, far1)
    arrive(fields_far)
    moving, after = [], []
    for outs in (OUTER, INNER):
        span = slice(outs[0], outs[-1] + 1)
        part = evaluate(False, far1, tuple(t[span] for t in sums), outs, outs != OUTER)
        new = finish(own1, part, drain[span], [t[span] for t in velocity], outs)
        for plane in range(3):
            own2[plane, span, 0:ROWS, :] = new[plane]
            own2[plane, span, ROWS : 2 * ROWS, :] = new[plane]
        after.append(new[3:])
        moving += send_straight(own2, far2, fields, pl.ds(outs[0], len(outs)))
        if outs == OUTER:
            pack(own2, 3, 1)
            moving += send_corners(1)
            rim2 = send_across(own2)
    velocity = [jnp.concatenate(pair, axis=0) for pair in zip(*after)]

    arrive(rim2)
    duplicate_rim(own2, range(3))
    centre(own2)
    sums = evaluate(True, own2, (zero,) * 3)
    sums = evaluate(False, None, sums, ends="near")
    finish_sends(len(messages) - 7)
    arrive(moving)
    unpack(far2, 3, 1)
    sums = evaluate(False, far2, sums, ends="far")
    n0, n1, np_, v0, v1 = finish(own2, sums, drain, velocity)

    for k, j in enumerate(PLACES):
        at = slice(j * LANES, (j + 1) * LANES)
        out_disp[0, :, at] = n0[k]
        out_disp[1, :, at] = n1[k]
        out_vel[0, :, at] = v0[k]
        out_vel[1, :, at] = v1[k]
        out_pres[:, at] = np_[k]

    finish_sends(len(messages))


def hand_over(a, b, c, out_a, out_b, out_c, sems):
    copies = [
        pltpu.make_async_copy(source, target, sems.at[i])
        for i, (source, target) in enumerate(((a, out_a), (b, out_b), (c, out_c)))
    ]
    for copy in copies:
        copy.start()
    for copy in copies:
        copy.wait()


def body(gx_count, displacement, velocity, pressure, broken_bits, material_class, table):
    height, breadth = pressure.shape
    assert height == ROWS and breadth % LANES == 0 and breadth == len(PLACES) * LANES
    blocks = breadth // LANES
    vmem = pl.BlockSpec(memory_space=pltpu.VMEM)
    anywhere = pl.BlockSpec(memory_space=pltpu.HBM)
    f, i32 = jnp.float32, jnp.int32
    dma = pltpu.SemaphoreType.DMA
    n_own, n_far = (len(SLOTS[own]) for own in (True, False))

    def planes(n, blocks, rows):
        return pltpu.VMEM((n, blocks, rows, LANES), f)

    shapes = (displacement.shape, velocity.shape, pressure.shape)
    results = pl.pallas_call(
        functools.partial(kernel, gx_count),
        out_shape=tuple(pltpu.VMEM(s, f) for s in shapes),
        in_specs=[anywhere] * 6,
        out_specs=(vmem, vmem, vmem),
        scratch_shapes=[
            pltpu.VMEM(displacement.shape, f),
            pltpu.VMEM(velocity.shape, f),
            pltpu.VMEM(pressure.shape, f),
            pltpu.VMEM(broken_bits.shape, i32),
            pltpu.VMEM(material_class.shape, i32),
            pltpu.SMEM(table.shape, f),
            planes(4, blocks + 1, 2 * ROWS),
            planes(4, blocks + 1, 2 * ROWS),
            planes(3, blocks + 1, 2 * ROWS),
            planes(3, blocks + 1, 2 * ROWS),
            pltpu.VMEM((2, ROWS, LANES), f),
            pltpu.VMEM((2, 2 * ROWS, LANES), f),
            planes(SPAN, blocks + 1, 2 * ROWS),
            planes(SPAN, blocks + 1, 2 * ROWS),
            planes(SPAN, blocks, 2 * ROWS),
            planes(SPAN, blocks, 2 * ROWS),
            pltpu.VMEM((2, SPAN, blocks, 2 * ROWS, LANES), f),
            pltpu.VMEM((2, SPAN, blocks, 2 * ROWS, LANES), f),
            planes(2, table.shape[0], ROWS),
            planes(2, blocks, ROWS),
            planes(n_own, blocks, ROWS),
            planes(n_own, blocks, ROWS),
            planes(n_far, blocks, ROWS),
            planes(n_far, blocks, ROWS),
            planes(n_own, blocks, ROWS),
            planes(n_far, blocks, ROWS),
            planes(Y_SLOTS, blocks + 1, ROWS),
            planes(Y_SLOTS, blocks + 1, ROWS),
            planes(SPAN, blocks, ROWS),
            planes(2, blocks, ROWS),
            dma((6,)), dma((MESSAGES,)), dma((MESSAGES,)),
        ],
        compiler_params=pltpu.CompilerParams(
            collective_id=0, has_side_effects=True, vmem_limit_bytes=62 * 1024 * 1024
        ),
        name="peridynamics",
    )(displacement, velocity, pressure, broken_bits, material_class, table)
    return pl.pallas_call(
        hand_over,
        out_shape=tuple(jax.ShapeDtypeStruct(s, f) for s in shapes),
        in_specs=[vmem] * 3,
        out_specs=(anywhere,) * 3,
        scratch_shapes=[dma((3,))],
        name="hand_over",
    )(*[pltpu.with_memory_space_constraint(r, pltpu.VMEM) for r in results])


def solution(mesh):
    plane = P(("sample", "gx"), "gy")
    stack = P(None, ("sample", "gx"), "gy")
    assert mesh.shape["gy"] == 2
    return jax.shard_map(
        functools.partial(body, mesh.shape["gx"]),
        mesh=mesh,
        in_specs=(stack, stack, plane, stack, plane, P("sample", None)),
        out_specs=(stack, stack, plane),
        check_vma=False,
    )
```

```python
import functools
import math

import jax
import jax.numpy as jnp
from jax import lax
from jax.experimental import pallas as pl
from jax.experimental.pallas import tpu as pltpu
from jax.sharding import PartitionSpec as P

REACH = 6
SPAN = 2 * REACH + 1
MESH = pl.DeviceIdType.MESH
LANES = 128
ROWS = 8
OUTSIDE = -1
PLACES = (0, 3, 1, 2)
RIM = len(PLACES)
AFTER, BEFORE = (2, RIM, 3, 1), (RIM, 3, 0, 2)
OUTER, INNER, ALL = (0, 1), (2, 3), (0, 1, 2, 3)
MESSAGES = 14
STRIP = 16
HALF = 4
JOINED = (2, 3)
Y_SLOTS = ROWS + 3
FAR = 3.0e38

half_width = {a: math.isqrt(37 - a * a) for a in range(-REACH, REACH + 1)}
first_bond = {}
_count = 0
for _a in range(-REACH, REACH + 1):
    first_bond[_a] = _count
    _count += 2 * half_width[_a] + 1 - (1 if _a == 0 else 0)


def bond(a, b):
    if abs(a) > REACH or abs(b) > half_width[a] or (a == 0 and b == 0):
        return None
    return first_bond[a] + b + half_width[a] - (1 if a == 0 and b > 0 else 0)


def groups_of(own):
    offsets = range(ROWS) if own else range(2, ROWS - 1)
    out = [(o, o, o - ROWS if o else 0) if own else (o, o - ROWS, o) for o in offsets]
    return out if own else out + [(-m, -m, m) for m in JOINED]


RING = 16


def columns_of(low, high):
    return max(half_width.get(low, -1), half_width.get(high, -1))


def slots_of(own):
    slots = {}
    for o, low, high in groups_of(own):
        widths = half_width.get(low, -1), half_width.get(high, -1)
        for b in range(-max(widths), max(widths) + 1):
            one_sided = abs(b) > min(widths)
            if not own and o > 0 and one_sided:
                continue
            if o < 0 and abs(b) <= half_width.get(ROWS + o, -1):
                continue
            if low or b:
                slots[o, b] = len(slots)
    return slots


SLOTS = {own: slots_of(own) for own in (True, False)}


def kernel(
    gx_count, disp, vel, pres, bits, klass, table,
    out_disp, out_vel, out_pres,
    disp_v, vel_v, pres_v, bits_v, klass_v, table_s,
    own1, far1, own2, far2, own_pack, far_pack,
    z_own, z_far, q_own, q_far, inv_own, inv_far, inverse, here_inv,
    w_own, v_own, w_far, v_far, ex_own, ex_far, y_own, y_far, side_b, still,
    ring1, ring2, ring_here, w_ring, v_ring, spread,
    local_sem, send_sem, recv_sem,
):
    f32 = jnp.float32
    sample, gx, gy = lax.axis_index("sample"), lax.axis_index("gx"), lax.axis_index("gy")
    height, breadth = pres.shape
    blocks = breadth // LANES
    has_up, has_down = gx > 0, gx < gx_count - 1
    up, down, mate = gx - 1, gx + 1, 1 - gy

    local = [
        pltpu.make_async_copy(table, table_s, local_sem.at[0]),
        pltpu.make_async_copy(klass, klass_v, local_sem.at[1]),
        pltpu.make_async_copy(disp, disp_v, local_sem.at[2]),
        pltpu.make_async_copy(pres, pres_v, local_sem.at[3]),
        pltpu.make_async_copy(bits, bits_v, local_sem.at[4]),
        pltpu.make_async_copy(vel, vel_v, local_sem.at[5]),
    ]
    for copy in local:
        copy.start()

    for plane in range(4):
        fill = float(OUTSIDE) if plane == 3 else 0.0
        far1[plane] = jnp.full(far1.shape[1:], fill, f32)
        if plane < 3:
            far2[plane] = jnp.zeros(far2.shape[1:], f32)
    far_pack[...] = jnp.full(far_pack.shape, float(OUTSIDE), f32)

    barrier = pltpu.get_barrier_semaphore()

    def greet(x, y):
        pl.semaphore_signal(barrier, inc=1, device_id=(sample, x, y), device_id_type=MESH)

    @pl.when(has_up)
    def _():
        greet(up, gy)
        greet(up, mate)

    @pl.when(has_down)
    def _():
        greet(down, gy)
        greet(down, mate)

    greet(gx, mate)

    def cut(value):
        return [value[:, j * LANES : (j + 1) * LANES] for j in PLACES]

    def put(target, plane, value):
        for j, piece in enumerate(cut(value)):
            for rows in (slice(0, ROWS), slice(ROWS, 2 * ROWS)):
                target[plane, j, rows, :] = piece

    for i in (1, 2, 3):
        local[i].wait()
    put(own1, 3, klass_v[...].astype(f32))
    put(own1, 0, disp_v[0])
    put(own1, 1, disp_v[1])
    put(own1, 2, pres_v[...])

    edge, rim = pl.ds(1 - gy, 1), pl.ds(RIM, 1)
    to_up = (pl.ds(0, REACH), pl.ds(ROWS, REACH))
    to_down = (pl.ds(ROWS - REACH, REACH), pl.ds(ROWS - REACH, REACH))
    routes = (
        (has_up, has_down, (sample, up, gy), to_up),
        (has_down, has_up, (sample, down, gy), to_down),
        (has_up, has_down, (sample, up, mate), to_up),
        (has_down, has_up, (sample, down, mate), to_down),
        (None, None, (sample, gx, mate), None),
    )
    STRAIGHT, CORNERS, ACROSS = (0, 1), (2, 3), (4,)
    messages = []

    def when(condition, act):
        if condition is None:
            act()
        else:
            pl.when(condition)(act)

    sublane = lax.broadcasted_iota(jnp.int32, (ROWS, LANES), 0)
    lane = lax.broadcasted_iota(jnp.int32, (ROWS, LANES), 1)

    def pack(x, planes, which):
        strip = ((lane - (1 - gy) * (LANES - STRIP)) & (LANES - 1)) >> 4
        total = None
        for plane in range(planes):
            value = x[plane, pl.ds(1 - gy, 1), 0:ROWS, :][0]
            if plane:
                total = jnp.where(strip == plane, pltpu.roll(value, STRIP * plane, 1), total)
            else:
                total = value
        own_pack[which] = total

    def unpack(x, planes, which):
        for rows in (slice(0, ROWS), slice(ROWS, 2 * ROWS)):
            value = far_pack[which, rows, :]
            for plane in range(planes):
                x[plane, RIM, rows, :] = (
                    pltpu.roll(value, LANES - STRIP * plane, 1) if plane else value
                )

    def send(routes_used, source, target):
        sent = []
        for n in routes_used:
            going, coming, device, rows = routes[n]
            here, there = (pl.ds(0, ROWS),) * 2 if rows is None else rows
            m = len(messages)
            copy = pltpu.make_async_remote_copy(
                src_ref=source(here), dst_ref=target(there),
                send_sem=send_sem.at[m], recv_sem=recv_sem.at[m],
                device_id=device, device_id_type=MESH,
            )
            when(going, copy.start)
            messages.append((going, copy))
            sent.append((coming, copy))
        return sent

    def send_straight(own, far, planes, blocks):
        return send(
            STRAIGHT, lambda r: own.at[planes, blocks, r], lambda r: far.at[planes, blocks, r]
        )

    def send_across(own):
        return send(ACROSS, lambda r: own.at[:, edge, r], lambda r: own.at[:, rim, r])

    def send_corners(which):
        return send(CORNERS, lambda r: own_pack.at[which, r], lambda r: far_pack.at[which, r])

    waited = []

    def finish_sends(count):
        for going, copy in messages[len(waited) : count]:
            when(going, copy.wait_send)
            waited.append(copy)

    def arrive(sent):
        for coming, copy in sent:
            when(coming, copy.wait_recv)

    pack(own1, 4, 0)
    pl.semaphore_wait(
        barrier, 1 + 2 * has_up.astype(jnp.int32) + 2 * has_down.astype(jnp.int32)
    )
    fields, kinds = pl.ds(0, 3), pl.ds(3, 1)
    four = pl.ds(0, blocks)
    four = pl.ds(0, blocks)
    kinds_far = send_straight(own1, far1, kinds, four) + send_corners(0)
    fields_far = send_straight(own1, far1, fields, four)
    rim1 = send_across(own1)

    def first_rows(o):
        return sublane < (ROWS - o if o >= 0 else -o)

    def mix(o, low, high, kind=f32):
        return kind(low) if low == high else jnp.where(first_rows(o), kind(low), kind(high))

    def window(get, o):
        if o >= 0:
            return get(pl.ds(o, ROWS))
        return jnp.where(first_rows(o), get(pl.ds(ROWS + o, ROWS)), get(pl.ds(-o, ROWS)))

    local[0].wait()

    def look_up(which, member):
        value = jnp.full(which.shape, table_s[table.shape[0] - 1, member], f32)
        for c in range(table.shape[0] - 1):
            value = jnp.where(which == c, table_s[c, member], value)
        return value

    classes = table.shape[0]
    for m in range(2):
        for c in range(classes):
            inverse[m, c] = 1.0 / jnp.full((ROWS, LANES), table_s[c, m], f32)

    def inverses(which):
        out = [jnp.full(which.shape, FAR, f32)] * 2
        for c in range(classes):
            chosen = which == float(c)
            out = [jnp.where(chosen, inverse[m, c], out[m]) for m in range(2)]
        return out

    for m, value in enumerate(inverses(own1[3, :blocks, 0:ROWS, :])):
        here_inv[m] = value

    klass_own = klass_v[...]
    for plane, member in ((0, 2), (1, 3)):
        for j, piece in enumerate(cut(look_up(klass_own, member))):
            still[plane, j] = piece
    local[4].wait()
    for j in range(blocks):
        words = [bits_v[w, :, PLACES[j] * LANES : (PLACES[j] + 1) * LANES] for w in range(bits.shape[0])]

        def broken(a, b):
            k = bond(a, b)
            return jnp.int32(1) if k is None else words[k // 12] & (1 << (k % 12))

        for own, w_to, v_to in ((True, w_own, v_own), (False, w_far, v_far)):
            for o, low, high in groups_of(own):
                for b in range(-columns_of(low, high), columns_of(low, high) + 1):
                    if (o, b) not in SLOTS[own]:
                        continue
                    n = SLOTS[own][o, b]
                    one = broken(low, b)
                    if low != high:
                        one = jnp.where(first_rows(o), one, broken(high, b))
                    if o < 0:
                        one = jnp.where((sublane >= -o) & (sublane < ROWS + o), 1, one)
                    squares = [a * a + b * b for a in (low, high)]
                    w_to[n, j] = jnp.where(one == 0, mix(o, *[2.0 / x**2 for x in squares]), 0.0)
                    v_to[n, j] = jnp.where(one == 0, mix(o, *[2.0 / x for x in squares]), 0.0)

    def load(get, which):
        runs = []
        for k in which:
            if runs and runs[-1][1] == k:
                runs[-1][1] = k + 1
            else:
                runs.append([k, k + 1])
        pieces = [get(*run) for run in runs]
        return pieces[0] if len(pieces) == 1 else jnp.concatenate(pieces, axis=0)

    def shift(get, b, outs=ALL):
        if b == 0:
            return load(get, outs)
        other = [(AFTER if b > 0 else BEFORE)[k] for k in outs]
        sources = sorted(set(outs) | set(other))
        turned = pltpu.roll(load(get, sources), (-b) % LANES, 2)

        def take(which):
            at = [sources.index(k) for k in which]
            return load(lambda i, j: turned[i:j], at)

        return jnp.where(lane < LANES - b if b > 0 else lane >= -b, take(outs), take(other))

    def tiles(own):
        top, bottom = slice(0, ROWS), slice(ROWS, 2 * ROWS)
        return [(top, (top, bottom))] if own else [(top, (top,)), (bottom, (bottom,))]

    valid = (lane < LANES // 2) == (gy == 0)

    def weigh(own, x):
        w_ref, v_ref, inv = (w_own, v_own, inv_own) if own else (w_far, v_far, inv_far)
        known = []
        for read, write in tiles(own):
            value = x[3, :, read, :]
            rim_value = jnp.where(valid, value[blocks:], float(OUTSIDE))
            known.append(inverses(jnp.concatenate([value[:blocks], rim_value], axis=0)))
        if not own:
            for m in range(2):
                top, bottom = known[0][m], known[1][m]
                for i, k in enumerate(spots):
                    at = slice(2 * i, 2 * i + 1)
                    ring1[3 + m, at, :] = top[k, ROWS - 1 : ROWS]
                    ring1[3 + m, 2 * i + 1 : 2 * i + 2, :] = bottom[k, 0:1]
        drain = jnp.zeros((blocks, ROWS, LANES), f32)
        for b in sorted(range(-REACH, REACH + 1), key=abs):
            for (read, write), pair in zip(tiles(own), known):
                for m, value in enumerate(pair):
                    moved = shift(lambda i, j: value[i:j], b)
                    for rows in write:
                        inv[m, b + REACH, :, rows, :] = moved
            for o, low, high in groups_of(own):
                if (o, b) not in SLOTS[own]:
                    continue
                n = SLOTS[own][o, b]
                cubes = [0.25 * math.sqrt(a * a + b * b) ** 3 for a in (low, high)]
                weight, flow = (
                    ref[n]
                    * pl.reciprocal(
                        here_inv[m] + window(lambda r: inv[m, b + REACH, :, r, :], o),
                        approx=True,
                    )
                    for m, ref in enumerate((w_ref, v_ref))
                )
                share = mix(o, *cubes) * weight
                w_ref[n] = weight
                v_ref[n] = flow - share
                drain = drain + (flow + share)
        return drain

    def centre(x):
        u, v, p = (x[plane, :blocks, 0:ROWS, :] for plane in range(3))
        for b in range(-REACH, REACH + 1):
            side_b[b + REACH] = float(b) * v + (0.25 * b * b) * p
        for own, target in ((True, ex_own), (False, ex_far)):
            for o, low, high in groups_of(own):
                here = mix(o, low, high) * u + mix(o, 0.25 * low * low, 0.25 * high * high) * p
                for b in range(-columns_of(low, high), columns_of(low, high) + 1):
                    if (o, b) in SLOTS[own]:
                        target[SLOTS[own][o, b]] = here if b == 0 else here + side_b[b + REACH]

    def evaluate(own, x, sums, outs=ALL, ready=False, ends="both"):
        w_ref, v_ref, ex, z, q_moved, y = (
            (w_own, v_own, ex_own, z_own, q_own, y_own)
            if own
            else (w_far, v_far, ex_far, z_far, q_far, y_far)
        )
        slots = SLOTS[own]
        force_x, force_y, gain = sums
        span = slice(outs[0], outs[-1] + 1)
        ready = ready or ends == "near"
        if not ready:
            for o, low, high in groups_of(own):
                if low:
                    u, q = (window(lambda r: x[m, :, r, :], o) for m in (0, 2))
                    y[o % Y_SLOTS] = (
                        mix(o, low, high) * u
                        - mix(o, 0.25 * low * low, 0.25 * high * high) * q
                    )
        groups = groups_of(own)
        sets = (groups,) if len(outs) < len(ALL) else (groups[: HALF], groups[HALF:])
        for chosen in sets:
            row_sums = {}
            for b in range(REACH + 1):
                if not ready and chosen is sets[0]:
                    for read, write in tiles(own):
                        if b:
                            v, q = x[1, :, read, :], x[2, :, read, :]
                            bv, bq = float(b) * v, (-0.25 * b * b) * q
                            for rows in write:
                                z[REACH + b, :, rows, :] = bq + bv
                                z[REACH - b, :, rows, :] = bq - bv
                        for c in (b, -b) if b else (0,):
                            moved = shift(lambda i, j: x[2, i:j, read, :], c)
                            for rows in write:
                                q_moved[c + REACH, :, rows, :] = moved
                side_sum = None
                for o, low, high in chosen:
                    if (o, b) not in slots:
                        continue
                    def one(c):
                        n = slots[o, c]

                        def there(i, j):
                            if c == 0:
                                return y[o % Y_SLOTS, i:j]
                            side = window(lambda r: z[c + REACH, i:j, r, :], o)
                            return side + y[o % Y_SLOTS, i:j] if low else side

                        if ends == "near":
                            return w_ref[n, span] * ex[n, span], None
                        far = shift(there, c, outs)
                        mag = w_ref[n, span] * (far - ex[n, span] if ends == "both" else far)
                        moved = window(lambda r: q_moved[c + REACH, span, r, :], o)
                        return mag, v_ref[n, span] * moved

                    def add(total, value):
                        return value if total is None else total + value

                    length = mix(o, *[math.sqrt(a * a + b * b) for a in (low, high)])
                    mag, flow = one(b)
                    if b:
                        mag2, flow2 = one(-b)
                        side_sum = add(side_sum, mag - mag2)
                        mag = mag + mag2
                    if low:
                        row_sums[o] = add(row_sums.get(o), mag)
                    if ends == "near":
                        gain = gain + length * mag
                        continue
                    gain = gain - length * mag + flow
                    if b:
                        gain = gain + flow2
                if side_sum is not None:
                    force_y = force_y - float(b) * side_sum if ends == "near" else force_y + float(b) * side_sum
            for o, low, high in chosen:
                if low:
                    part = mix(o, low, high) * row_sums[o]
                    force_x = force_x - part if ends == "near" else force_x + part
        return force_x, force_y, gain

    def duplicate_rim(x, planes):
        for plane in planes:
            x[plane, RIM, ROWS : 2 * ROWS, :] = x[plane, RIM, 0:ROWS, :]

    def finish(x, sums, drain, velocity, outs=ALL):
        span = slice(outs[0], outs[-1] + 1)
        force_x, force_y, gain = sums
        u0, u1, p = (x[plane, span, 0:ROWS, :] for plane in range(3))
        density, storage = still[0, span], still[1, span]
        v0 = velocity[0] + 0.1 * (density * force_x - 0.5 * velocity[0])
        v1 = velocity[1] + 0.1 * (density * force_y - 0.5 * velocity[1])
        pressure = p + 0.1 * storage * 0.1 * (gain - drain * p)
        return u0 + 0.1 * v0, u1 + 0.1 * v1, pressure, v0, v1

    spots = [RIM] + [PLACES.index(j) for j in range(blocks)] + [RIM]
    odd = (sublane & 1) == 1
    step_a = jnp.where(odd, 1.0, -1.0)

    def fill_ring(ring, plane, get):
        for i, k in enumerate(spots):
            ring[plane, 2 * i : 2 * i + 1, :] = get(k, ROWS - 1)
            ring[plane, 2 * i + 1 : 2 * i + 2, :] = get(k, ROWS)

    def ring_fields(ring, far):
        for plane in range(3):
            fill_ring(ring, plane, lambda k, r: far[plane, k, r : r + 1, :])

    def ring_centre(plane, get):
        for j in range(blocks):
            k = PLACES.index(j)
            ring_here[plane, 2 * j : 2 * j + 1, :] = get(k, 0)
            ring_here[plane, 2 * j + 1 : 2 * j + 2, :] = get(k, ROWS - 1)

    def ring_masks():
        for b in range(-REACH, REACH + 1):
            for ref, scale in ((w_ring, 2.0 / (1 + b * b) ** 2), (v_ring, 2.0 / (1 + b * b))):
                for j in range(blocks):
                    for i, (a, r) in enumerate(((-1, 0), (1, ROWS - 1))):
                        k = bond(a, b)
                        word = bits_v[k // 12, r : r + 1, j * LANES : (j + 1) * LANES]
                        ref[b + REACH, 2 * j + i : 2 * j + i + 1, :] = jnp.where(
                            (word & (1 << (k % 12))) == 0, scale, 0.0
                        )

    MAIN = pl.ds(2, ROWS)

    def ring_shift(get, b):
        if b == 0:
            return get(MAIN)
        other = pl.ds(4, ROWS) if b > 0 else pl.ds(0, ROWS)
        mine, next_to = (pltpu.roll(get(r), (-b) % LANES, 1) for r in (MAIN, other))
        return jnp.where(lane < LANES - b if b > 0 else lane >= -b, mine, next_to)

    def ring_weigh():
        drain = jnp.zeros((ROWS, LANES), f32)
        for b in range(-REACH, REACH + 1):
            weight, flow = (
                ref[b + REACH]
                * pl.reciprocal(
                    ring_here[3 + m] + ring_shift(lambda r: ring1[3 + m, r, :], b), approx=True
                )
                for m, ref in enumerate((w_ring, v_ring))
            )
            share = (0.25 * math.sqrt(1 + b * b) ** 3) * weight
            w_ring[b + REACH] = weight
            v_ring[b + REACH] = flow - share
            drain = drain + (flow + share)
        return drain

    def ring_sums(ring):
        u, v, p = (ring_here[plane] for plane in range(3))
        near = step_a * u + 0.25 * p
        force_x = force_y = gain = pull = jnp.zeros((ROWS, LANES), f32)
        for b in range(-REACH, REACH + 1):
            def there(r):
                value = step_a * ring[0, r, :] - (0.25 + 0.25 * b * b) * ring[2, r, :]
                return value + float(b) * ring[1, r, :] if b else value

            mine = near + (float(b) * v + (0.25 * b * b) * p) if b else near
            mag = w_ring[b + REACH] * (ring_shift(there, b) - mine)
            gain = gain + v_ring[b + REACH] * ring_shift(lambda r: ring[2, r, :], b)
            pull = pull + math.sqrt(1 + b * b) * mag
            force_x = force_x + mag
            force_y = force_y + float(b) * mag
        return step_a * force_x, force_y, gain - pull

    def unring(values):
        out = []
        for i, value in enumerate(values):
            spread[i] = value
            parts = []
            for j in PLACES:
                first, last = (
                    jnp.broadcast_to(spread[i, 2 * j + e : 2 * j + e + 1, :], (ROWS, LANES))
                    for e in (0, 1)
                )
                parts.append(
                    jnp.where(sublane == 0, first, jnp.where(sublane == ROWS - 1, last, 0.0))
                )
            out.append(jnp.stack(parts))
        return out

    def with_ring(sums, ring):
        return tuple(t + r for t, r in zip(sums, unring(ring_sums(ring))))

    zero = jnp.zeros((blocks, ROWS, LANES), f32)

    arrive(rim1)
    duplicate_rim(own1, range(4))
    drain = weigh(True, own1)
    centre(own1)
    ring_masks()
    for plane in range(3):
        ring_centre(plane, lambda k, r: own1[plane, k, r : r + 1, :])
    for m in range(2):
        ring_centre(3 + m, lambda k, r: here_inv[m, k, r : r + 1, :])
    sums = evaluate(True, own1, (zero,) * 3)
    local[5].wait()
    velocity = [jnp.stack(cut(vel_v[i])) for i in range(2)]

    arrive(kinds_far)
    unpack(far1, 4, 0)
    drain = drain + weigh(False, far1)
    drain = drain + unring([ring_weigh()])[0]
    arrive(fields_far)
    ring_fields(ring1, far1)
    moving, after = [], []
    for outs in (ALL,):
        span = slice(outs[0], outs[-1] + 1)
        part = with_ring(evaluate(False, far1, sums), ring1)
        new = finish(own1, part, drain[span], [t[span] for t in velocity], outs)
        for plane in range(3):
            own2[plane, span, 0:ROWS, :] = new[plane]
            own2[plane, span, ROWS : 2 * ROWS, :] = new[plane]
        after.append(new[3:])
        moving += send_straight(own2, far2, fields, pl.ds(outs[0], len(outs)))
        if True:
            pack(own2, 3, 1)
            moving += send_corners(1)
            rim2 = send_across(own2)
    velocity = [jnp.concatenate(pair, axis=0) for pair in zip(*after)]

    arrive(rim2)
    duplicate_rim(own2, range(3))
    centre(own2)
    sums = evaluate(True, own2, (zero,) * 3)
    sums = evaluate(False, None, sums, ends="near")
    for plane in range(3):
        ring_centre(plane, lambda k, r: own2[plane, k, r : r + 1, :])
    finish_sends(7)
    arrive(moving)
    unpack(far2, 3, 1)
    ring_fields(ring2, far2)
    sums = evaluate(False, far2, sums, ends="far")
    sums = with_ring(sums, ring2)
    n0, n1, np_, v0, v1 = finish(own2, sums, drain, velocity)

    for k, j in enumerate(PLACES):
        at = slice(j * LANES, (j + 1) * LANES)
        out_disp[0, :, at] = n0[k]
        out_disp[1, :, at] = n1[k]
        out_vel[0, :, at] = v0[k]
        out_vel[1, :, at] = v1[k]
        out_pres[:, at] = np_[k]

    finish_sends(len(messages))


def hand_over(a, b, c, out_a, out_b, out_c, sems):
    copies = [
        pltpu.make_async_copy(source, target, sems.at[i])
        for i, (source, target) in enumerate(((a, out_a), (b, out_b), (c, out_c)))
    ]
    for copy in copies:
        copy.start()
    for copy in copies:
        copy.wait()


def body(gx_count, displacement, velocity, pressure, broken_bits, material_class, table):
    height, breadth = pressure.shape
    assert height == ROWS and breadth % LANES == 0 and breadth == len(PLACES) * LANES
    blocks = breadth // LANES
    vmem = pl.BlockSpec(memory_space=pltpu.VMEM)
    anywhere = pl.BlockSpec(memory_space=pltpu.HBM)
    f, i32 = jnp.float32, jnp.int32
    dma = pltpu.SemaphoreType.DMA
    n_own, n_far = (len(SLOTS[own]) for own in (True, False))

    def planes(n, blocks, rows):
        return pltpu.VMEM((n, blocks, rows, LANES), f)

    shapes = (displacement.shape, velocity.shape, pressure.shape)
    results = pl.pallas_call(
        functools.partial(kernel, gx_count),
        out_shape=tuple(pltpu.VMEM(s, f) for s in shapes),
        in_specs=[anywhere] * 6,
        out_specs=(vmem, vmem, vmem),
        scratch_shapes=[
            pltpu.VMEM(displacement.shape, f),
            pltpu.VMEM(velocity.shape, f),
            pltpu.VMEM(pressure.shape, f),
            pltpu.VMEM(broken_bits.shape, i32),
            pltpu.VMEM(material_class.shape, i32),
            pltpu.SMEM(table.shape, f),
            planes(4, blocks + 1, 2 * ROWS),
            planes(4, blocks + 1, 2 * ROWS),
            planes(3, blocks + 1, 2 * ROWS),
            planes(3, blocks + 1, 2 * ROWS),
            pltpu.VMEM((2, ROWS, LANES), f),
            pltpu.VMEM((2, 2 * ROWS, LANES), f),
            planes(SPAN, blocks + 1, 2 * ROWS),
            planes(SPAN, blocks + 1, 2 * ROWS),
            planes(SPAN, blocks, 2 * ROWS),
            planes(SPAN, blocks, 2 * ROWS),
            pltpu.VMEM((2, SPAN, blocks, 2 * ROWS, LANES), f),
            pltpu.VMEM((2, SPAN, blocks, 2 * ROWS, LANES), f),
            planes(2, table.shape[0], ROWS),
            planes(2, blocks, ROWS),
            planes(n_own, blocks, ROWS),
            planes(n_own, blocks, ROWS),
            planes(n_far, blocks, ROWS),
            planes(n_far, blocks, ROWS),
            planes(n_own, blocks, ROWS),
            planes(n_far, blocks, ROWS),
            planes(Y_SLOTS, blocks + 1, ROWS),
            planes(Y_SLOTS, blocks + 1, ROWS),
            planes(SPAN, blocks, ROWS),
            planes(2, blocks, ROWS),
            pltpu.VMEM((5, RING, LANES), f),
            pltpu.VMEM((5, RING, LANES), f),
            pltpu.VMEM((5, ROWS, LANES), f),
            pltpu.VMEM((SPAN, ROWS, LANES), f),
            pltpu.VMEM((SPAN, ROWS, LANES), f),
            pltpu.VMEM((3, ROWS, LANES), f),
            dma((6,)), dma((MESSAGES,)), dma((MESSAGES,)),
        ],
        compiler_params=pltpu.CompilerParams(
            collective_id=0, has_side_effects=True, vmem_limit_bytes=62 * 1024 * 1024
        ),
        name="peridynamics",
    )(displacement, velocity, pressure, broken_bits, material_class, table)
    return pl.pallas_call(
        hand_over,
        out_shape=tuple(jax.ShapeDtypeStruct(s, f) for s in shapes),
        in_specs=[vmem] * 3,
        out_specs=(anywhere,) * 3,
        scratch_shapes=[dma((3,))],
        name="hand_over",
    )(*[pltpu.with_memory_space_constraint(r, pltpu.VMEM) for r in results])


def solution(mesh):
    plane = P(("sample", "gx"), "gy")
    stack = P(None, ("sample", "gx"), "gy")
    assert mesh.shape["gy"] == 2
    return jax.shard_map(
        functools.partial(body, mesh.shape["gx"]),
        mesh=mesh,
        in_specs=(stack, stack, plane, stack, plane, P("sample", None)),
        out_specs=(stack, stack, plane),
        check_vma=False,
    )
```

```python
import functools
import math

import jax
import jax.numpy as jnp
from jax import lax
from jax.experimental import pallas as pl
from jax.experimental.pallas import tpu as pltpu
from jax.sharding import PartitionSpec as P

REACH = 6
SPAN = 2 * REACH + 1
MESH = pl.DeviceIdType.MESH
LANES = 128
ROWS = 8
OUTSIDE = -1
PLACES = (0, 3, 1, 2)
RIM = len(PLACES)
AFTER, BEFORE = (2, RIM, 3, 1), (RIM, 3, 0, 2)
OUTER, INNER, ALL = (0, 1), (2, 3), (0, 1, 2, 3)
MESSAGES = 14
STRIP = 16
HALF = 4
JOINED = (2, 3)
Y_SLOTS = ROWS + 3
FAR = 3.0e38

half_width = {a: math.isqrt(37 - a * a) for a in range(-REACH, REACH + 1)}
first_bond = {}
_count = 0
for _a in range(-REACH, REACH + 1):
    first_bond[_a] = _count
    _count += 2 * half_width[_a] + 1 - (1 if _a == 0 else 0)


def bond(a, b):
    if abs(a) > REACH or abs(b) > half_width[a] or (a == 0 and b == 0):
        return None
    return first_bond[a] + b + half_width[a] - (1 if a == 0 and b > 0 else 0)


def groups_of(own):
    offsets = range(ROWS) if own else range(2, ROWS - 1)
    out = [(o, o, o - ROWS if o else 0) if own else (o, o - ROWS, o) for o in offsets]
    return out if own else out + [(-m, -m, m) for m in JOINED]


RING = 16


def columns_of(low, high):
    return max(half_width.get(low, -1), half_width.get(high, -1))


def slots_of(own):
    slots = {}
    for o, low, high in groups_of(own):
        widths = half_width.get(low, -1), half_width.get(high, -1)
        for b in range(-max(widths), max(widths) + 1):
            one_sided = abs(b) > min(widths)
            if not own and o > 0 and one_sided:
                continue
            if o < 0 and abs(b) <= half_width.get(ROWS + o, -1):
                continue
            if low or b:
                slots[o, b] = len(slots)
    return slots


SLOTS = {own: slots_of(own) for own in (True, False)}


def kernel(
    gx_count, disp, vel, pres, bits, klass, table,
    out_disp, out_vel, out_pres,
    disp_v, vel_v, pres_v, bits_v, klass_v, table_s,
    own1, far1, own2, far2, own_pack, far_pack,
    z_own, z_far, q_own, q_far, inv_own, inv_far, inverse, here_inv,
    w_own, v_own, w_far, v_far, ex_own, ex_far, y_own, y_far, side_b, still,
    ring1, ring2, ring_here, w_ring, v_ring, spread,
    local_sem, send_sem, recv_sem,
):
    f32 = jnp.float32
    sample, gx, gy = lax.axis_index("sample"), lax.axis_index("gx"), lax.axis_index("gy")
    height, breadth = pres.shape
    blocks = breadth // LANES
    has_up, has_down = gx > 0, gx < gx_count - 1
    up, down, mate = gx - 1, gx + 1, 1 - gy

    barrier = pltpu.get_barrier_semaphore()

    def greet(x, y):
        pl.semaphore_signal(barrier, inc=1, device_id=(sample, x, y), device_id_type=MESH)

    @pl.when(has_up)
    def _():
        greet(up, gy)
        greet(up, mate)

    @pl.when(has_down)
    def _():
        greet(down, gy)
        greet(down, mate)

    greet(gx, mate)

    local = [
        pltpu.make_async_copy(table, table_s, local_sem.at[0]),
        pltpu.make_async_copy(klass, klass_v, local_sem.at[1]),
        pltpu.make_async_copy(disp, disp_v, local_sem.at[2]),
        pltpu.make_async_copy(pres, pres_v, local_sem.at[3]),
        pltpu.make_async_copy(bits, bits_v, local_sem.at[4]),
        pltpu.make_async_copy(vel, vel_v, local_sem.at[5]),
    ]
    for copy in local:
        copy.start()

    def clear(rows):
        count = rows.stop - rows.start
        for ref, planes in ((far1, 4), (far2, 3)):
            for plane in range(planes):
                fill = float(OUTSIDE) if plane == 3 else 0.0
                ref[plane, :blocks, rows, :] = jnp.full((blocks, count, LANES), fill, f32)
        far_pack[:, rows, :] = jnp.full((2, count, LANES), float(OUTSIDE), f32)

    clear(slice(0, ROWS - REACH))
    clear(slice(ROWS + REACH, 2 * ROWS))

    @pl.when(jnp.logical_not(has_up))
    def _():
        clear(slice(ROWS - REACH, ROWS))

    @pl.when(jnp.logical_not(has_down))
    def _():
        clear(slice(ROWS, ROWS + REACH))


    def cut(value):
        return [value[:, j * LANES : (j + 1) * LANES] for j in PLACES]

    def put(target, plane, value):
        for j, piece in enumerate(cut(value)):
            for rows in (slice(0, ROWS), slice(ROWS, 2 * ROWS)):
                target[plane, j, rows, :] = piece

    for i in (1, 2, 3):
        local[i].wait()
    put(own1, 3, klass_v[...].astype(f32))
    put(own1, 0, disp_v[0])
    put(own1, 1, disp_v[1])
    put(own1, 2, pres_v[...])

    edge, rim = pl.ds(1 - gy, 1), pl.ds(RIM, 1)
    to_up = (pl.ds(0, REACH), pl.ds(ROWS, REACH))
    to_down = (pl.ds(ROWS - REACH, REACH), pl.ds(ROWS - REACH, REACH))
    routes = (
        (has_up, has_down, (sample, up, gy), to_up),
        (has_down, has_up, (sample, down, gy), to_down),
        (has_up, has_down, (sample, up, mate), to_up),
        (has_down, has_up, (sample, down, mate), to_down),
        (None, None, (sample, gx, mate), None),
    )
    STRAIGHT, CORNERS, ACROSS = (0, 1), (2, 3), (4,)
    messages = []

    def when(condition, act):
        if condition is None:
            act()
        else:
            pl.when(condition)(act)

    sublane = lax.broadcasted_iota(jnp.int32, (ROWS, LANES), 0)
    lane = lax.broadcasted_iota(jnp.int32, (ROWS, LANES), 1)

    def pack(x, planes, which):
        strip = ((lane - (1 - gy) * (LANES - STRIP)) & (LANES - 1)) >> 4
        total = None
        for plane in range(planes):
            value = x[plane, pl.ds(1 - gy, 1), 0:ROWS, :][0]
            if plane:
                total = jnp.where(strip == plane, pltpu.roll(value, STRIP * plane, 1), total)
            else:
                total = value
        own_pack[which] = total

    def unpack(x, planes, which):
        for rows in (slice(0, ROWS), slice(ROWS, 2 * ROWS)):
            value = far_pack[which, rows, :]
            for plane in range(planes):
                x[plane, RIM, rows, :] = (
                    pltpu.roll(value, LANES - STRIP * plane, 1) if plane else value
                )

    def send(routes_used, source, target):
        sent = []
        for n in routes_used:
            going, coming, device, rows = routes[n]
            here, there = (pl.ds(0, ROWS),) * 2 if rows is None else rows
            m = len(messages)
            copy = pltpu.make_async_remote_copy(
                src_ref=source(here), dst_ref=target(there),
                send_sem=send_sem.at[m], recv_sem=recv_sem.at[m],
                device_id=device, device_id_type=MESH,
            )
            when(going, copy.start)
            messages.append((going, copy))
            sent.append((coming, copy))
        return sent

    def send_straight(own, far, planes, blocks):
        return send(
            STRAIGHT, lambda r: own.at[planes, blocks, r], lambda r: far.at[planes, blocks, r]
        )

    def send_across(own):
        return send(ACROSS, lambda r: own.at[:, edge, r], lambda r: own.at[:, rim, r])

    def send_corners(which):
        return send(CORNERS, lambda r: own_pack.at[which, r], lambda r: far_pack.at[which, r])

    waited = []

    def finish_sends(count):
        for going, copy in messages[len(waited) : count]:
            when(going, copy.wait_send)
            waited.append(copy)

    def arrive(sent):
        for coming, copy in sent:
            when(coming, copy.wait_recv)

    pack(own1, 4, 0)
    pl.semaphore_wait(
        barrier, 1 + 2 * has_up.astype(jnp.int32) + 2 * has_down.astype(jnp.int32)
    )
    fields, kinds = pl.ds(0, 3), pl.ds(3, 1)
    four = pl.ds(0, blocks)
    four = pl.ds(0, blocks)
    kinds_far = send_straight(own1, far1, kinds, four) + send_corners(0)
    fields_far = send_straight(own1, far1, fields, four)
    rim1 = send_across(own1)

    def first_rows(o):
        return sublane < (ROWS - o if o >= 0 else -o)

    def mix(o, low, high, kind=f32):
        return kind(low) if low == high else jnp.where(first_rows(o), kind(low), kind(high))

    def window(get, o):
        if o >= 0:
            return get(pl.ds(o, ROWS))
        return jnp.where(first_rows(o), get(pl.ds(ROWS + o, ROWS)), get(pl.ds(-o, ROWS)))

    local[0].wait()

    def look_up(which, member):
        value = jnp.full(which.shape, table_s[table.shape[0] - 1, member], f32)
        for c in range(table.shape[0] - 1):
            value = jnp.where(which == c, table_s[c, member], value)
        return value

    classes = table.shape[0]
    for m in range(2):
        for c in range(classes):
            inverse[m, c] = 1.0 / jnp.full((ROWS, LANES), table_s[c, m], f32)

    def inverses(which):
        out = [jnp.full(which.shape, FAR, f32)] * 2
        for c in range(classes):
            chosen = which == float(c)
            out = [jnp.where(chosen, inverse[m, c], out[m]) for m in range(2)]
        return out

    for m, value in enumerate(inverses(own1[3, :blocks, 0:ROWS, :])):
        here_inv[m] = value

    klass_own = klass_v[...]
    for plane, member in ((0, 2), (1, 3)):
        for j, piece in enumerate(cut(look_up(klass_own, member))):
            still[plane, j] = piece
    local[4].wait()
    for j in range(blocks):
        words = [bits_v[w, :, PLACES[j] * LANES : (PLACES[j] + 1) * LANES] for w in range(bits.shape[0])]

        def broken(a, b):
            k = bond(a, b)
            return jnp.int32(1) if k is None else words[k // 12] & (1 << (k % 12))

        for own, w_to, v_to in ((True, w_own, v_own), (False, w_far, v_far)):
            for o, low, high in groups_of(own):
                for b in range(-columns_of(low, high), columns_of(low, high) + 1):
                    if (o, b) not in SLOTS[own]:
                        continue
                    n = SLOTS[own][o, b]
                    one = broken(low, b)
                    if low != high:
                        one = jnp.where(first_rows(o), one, broken(high, b))
                    if o < 0:
                        one = jnp.where((sublane >= -o) & (sublane < ROWS + o), 1, one)
                    squares = [a * a + b * b for a in (low, high)]
                    w_to[n, j] = jnp.where(one == 0, mix(o, *[2.0 / x**2 for x in squares]), 0.0)
                    v_to[n, j] = jnp.where(one == 0, mix(o, *[2.0 / x for x in squares]), 0.0)

    def load(get, which):
        runs = []
        for k in which:
            if runs and runs[-1][1] == k:
                runs[-1][1] = k + 1
            else:
                runs.append([k, k + 1])
        pieces = [get(*run) for run in runs]
        return pieces[0] if len(pieces) == 1 else jnp.concatenate(pieces, axis=0)

    def shift(get, b, outs=ALL):
        if b == 0:
            return load(get, outs)
        other = [(AFTER if b > 0 else BEFORE)[k] for k in outs]
        sources = sorted(set(outs) | set(other))
        turned = pltpu.roll(load(get, sources), (-b) % LANES, 2)

        def take(which):
            at = [sources.index(k) for k in which]
            return load(lambda i, j: turned[i:j], at)

        return jnp.where(lane < LANES - b if b > 0 else lane >= -b, take(outs), take(other))

    def tiles(own):
        top, bottom = slice(0, ROWS), slice(ROWS, 2 * ROWS)
        return [(top, (top, bottom))] if own else [(top, (top,)), (bottom, (bottom,))]

    valid = (lane < LANES // 2) == (gy == 0)

    def weigh(own, x):
        w_ref, v_ref, inv = (w_own, v_own, inv_own) if own else (w_far, v_far, inv_far)
        known = []
        for read, write in tiles(own):
            value = x[3, :, read, :]
            rim_value = jnp.where(valid, value[blocks:], float(OUTSIDE))
            known.append(inverses(jnp.concatenate([value[:blocks], rim_value], axis=0)))
        if not own:
            for m in range(2):
                top, bottom = known[0][m], known[1][m]
                for i, k in enumerate(spots):
                    at = slice(2 * i, 2 * i + 1)
                    ring1[3 + m, at, :] = top[k, ROWS - 1 : ROWS]
                    ring1[3 + m, 2 * i + 1 : 2 * i + 2, :] = bottom[k, 0:1]
        drain = jnp.zeros((blocks, ROWS, LANES), f32)
        for b in sorted(range(-REACH, REACH + 1), key=abs):
            for (read, write), pair in zip(tiles(own), known):
                for m, value in enumerate(pair):
                    moved = shift(lambda i, j: value[i:j], b)
                    for rows in write:
                        inv[m, b + REACH, :, rows, :] = moved
            for o, low, high in groups_of(own):
                if (o, b) not in SLOTS[own]:
                    continue
                n = SLOTS[own][o, b]
                cubes = [0.25 * math.sqrt(a * a + b * b) ** 3 for a in (low, high)]
                weight, flow = (
                    ref[n]
                    * pl.reciprocal(
                        here_inv[m] + window(lambda r: inv[m, b + REACH, :, r, :], o),
                        approx=True,
                    )
                    for m, ref in enumerate((w_ref, v_ref))
                )
                share = mix(o, *cubes) * weight
                w_ref[n] = weight
                v_ref[n] = flow - share
                drain = drain + (flow + share)
        return drain

    def centre(x):
        u, v, p = (x[plane, :blocks, 0:ROWS, :] for plane in range(3))
        for b in range(-REACH, REACH + 1):
            side_b[b + REACH] = float(b) * v + (0.25 * b * b) * p
        for own, target in ((True, ex_own), (False, ex_far)):
            for o, low, high in groups_of(own):
                here = mix(o, low, high) * u + mix(o, 0.25 * low * low, 0.25 * high * high) * p
                for b in range(-columns_of(low, high), columns_of(low, high) + 1):
                    if (o, b) in SLOTS[own]:
                        target[SLOTS[own][o, b]] = here if b == 0 else here + side_b[b + REACH]

    def evaluate(own, x, sums, outs=ALL, ready=False, ends="both"):
        w_ref, v_ref, ex, z, q_moved, y = (
            (w_own, v_own, ex_own, z_own, q_own, y_own)
            if own
            else (w_far, v_far, ex_far, z_far, q_far, y_far)
        )
        slots = SLOTS[own]
        force_x, force_y, gain = sums
        span = slice(outs[0], outs[-1] + 1)
        ready = ready or ends == "near"
        if not ready:
            for o, low, high in groups_of(own):
                if low:
                    u, q = (window(lambda r: x[m, :, r, :], o) for m in (0, 2))
                    y[o % Y_SLOTS] = (
                        mix(o, low, high) * u
                        - mix(o, 0.25 * low * low, 0.25 * high * high) * q
                    )
        groups = groups_of(own)
        sets = (groups,) if len(outs) < len(ALL) else (groups[: HALF], groups[HALF:])
        for chosen in sets:
            row_sums = {}
            for b in range(REACH + 1):
                if not ready and chosen is sets[0]:
                    for read, write in tiles(own):
                        if b:
                            v, q = x[1, :, read, :], x[2, :, read, :]
                            bv, bq = float(b) * v, (-0.25 * b * b) * q
                            for rows in write:
                                z[REACH + b, :, rows, :] = bq + bv
                                z[REACH - b, :, rows, :] = bq - bv
                        for c in (b, -b) if b else (0,):
                            moved = shift(lambda i, j: x[2, i:j, read, :], c)
                            for rows in write:
                                q_moved[c + REACH, :, rows, :] = moved
                side_sum = None
                for o, low, high in chosen:
                    if (o, b) not in slots:
                        continue
                    def one(c):
                        n = slots[o, c]

                        def there(i, j):
                            if c == 0:
                                return y[o % Y_SLOTS, i:j]
                            side = window(lambda r: z[c + REACH, i:j, r, :], o)
                            return side + y[o % Y_SLOTS, i:j] if low else side

                        if ends == "near":
                            return w_ref[n, span] * ex[n, span], None
                        far = shift(there, c, outs)
                        mag = w_ref[n, span] * (far - ex[n, span] if ends == "both" else far)
                        moved = window(lambda r: q_moved[c + REACH, span, r, :], o)
                        return mag, v_ref[n, span] * moved

                    def add(total, value):
                        return value if total is None else total + value

                    length = mix(o, *[math.sqrt(a * a + b * b) for a in (low, high)])
                    mag, flow = one(b)
                    if b:
                        mag2, flow2 = one(-b)
                        side_sum = add(side_sum, mag - mag2)
                        mag = mag + mag2
                    if low:
                        row_sums[o] = add(row_sums.get(o), mag)
                    if ends == "near":
                        gain = gain + length * mag
                        continue
                    gain = gain - length * mag + flow
                    if b:
                        gain = gain + flow2
                if side_sum is not None:
                    force_y = force_y - float(b) * side_sum if ends == "near" else force_y + float(b) * side_sum
            for o, low, high in chosen:
                if low:
                    part = mix(o, low, high) * row_sums[o]
                    force_x = force_x - part if ends == "near" else force_x + part
        return force_x, force_y, gain

    def duplicate_rim(x, planes):
        for plane in planes:
            x[plane, RIM, ROWS : 2 * ROWS, :] = x[plane, RIM, 0:ROWS, :]

    def finish(x, sums, drain, velocity, outs=ALL):
        span = slice(outs[0], outs[-1] + 1)
        force_x, force_y, gain = sums
        u0, u1, p = (x[plane, span, 0:ROWS, :] for plane in range(3))
        density, storage = still[0, span], still[1, span]
        v0 = velocity[0] + 0.1 * (density * force_x - 0.5 * velocity[0])
        v1 = velocity[1] + 0.1 * (density * force_y - 0.5 * velocity[1])
        pressure = p + 0.1 * storage * 0.1 * (gain - drain * p)
        return u0 + 0.1 * v0, u1 + 0.1 * v1, pressure, v0, v1

    spots = [RIM] + [PLACES.index(j) for j in range(blocks)] + [RIM]
    odd = (sublane & 1) == 1
    step_a = jnp.where(odd, 1.0, -1.0)

    def fill_ring(ring, plane, get):
        for i, k in enumerate(spots):
            ring[plane, 2 * i : 2 * i + 1, :] = get(k, ROWS - 1)
            ring[plane, 2 * i + 1 : 2 * i + 2, :] = get(k, ROWS)

    def ring_fields(ring, far):
        for plane in range(3):
            fill_ring(ring, plane, lambda k, r: far[plane, k, r : r + 1, :])

    def ring_centre(plane, get):
        for j in range(blocks):
            k = PLACES.index(j)
            ring_here[plane, 2 * j : 2 * j + 1, :] = get(k, 0)
            ring_here[plane, 2 * j + 1 : 2 * j + 2, :] = get(k, ROWS - 1)

    def ring_masks():
        for b in range(-REACH, REACH + 1):
            for ref, scale in ((w_ring, 2.0 / (1 + b * b) ** 2), (v_ring, 2.0 / (1 + b * b))):
                for j in range(blocks):
                    for i, (a, r) in enumerate(((-1, 0), (1, ROWS - 1))):
                        k = bond(a, b)
                        word = bits_v[k // 12, r : r + 1, j * LANES : (j + 1) * LANES]
                        ref[b + REACH, 2 * j + i : 2 * j + i + 1, :] = jnp.where(
                            (word & (1 << (k % 12))) == 0, scale, 0.0
                        )

    MAIN = pl.ds(2, ROWS)

    def ring_shift(get, b):
        if b == 0:
            return get(MAIN)
        other = pl.ds(4, ROWS) if b > 0 else pl.ds(0, ROWS)
        mine, next_to = (pltpu.roll(get(r), (-b) % LANES, 1) for r in (MAIN, other))
        return jnp.where(lane < LANES - b if b > 0 else lane >= -b, mine, next_to)

    def ring_weigh():
        drain = jnp.zeros((ROWS, LANES), f32)
        for b in range(-REACH, REACH + 1):
            weight, flow = (
                ref[b + REACH]
                * pl.reciprocal(
                    ring_here[3 + m] + ring_shift(lambda r: ring1[3 + m, r, :], b), approx=True
                )
                for m, ref in enumerate((w_ring, v_ring))
            )
            share = (0.25 * math.sqrt(1 + b * b) ** 3) * weight
            w_ring[b + REACH] = weight
            v_ring[b + REACH] = flow - share
            drain = drain + (flow + share)
        return drain

    def ring_sums(ring):
        u, v, p = (ring_here[plane] for plane in range(3))
        near = step_a * u + 0.25 * p
        force_x = force_y = gain = pull = jnp.zeros((ROWS, LANES), f32)
        for b in range(-REACH, REACH + 1):
            def there(r):
                value = step_a * ring[0, r, :] - (0.25 + 0.25 * b * b) * ring[2, r, :]
                return value + float(b) * ring[1, r, :] if b else value

            mine = near + (float(b) * v + (0.25 * b * b) * p) if b else near
            mag = w_ring[b + REACH] * (ring_shift(there, b) - mine)
            gain = gain + v_ring[b + REACH] * ring_shift(lambda r: ring[2, r, :], b)
            pull = pull + math.sqrt(1 + b * b) * mag
            force_x = force_x + mag
            force_y = force_y + float(b) * mag
        return step_a * force_x, force_y, gain - pull

    def unring(values):
        out = []
        for i, value in enumerate(values):
            spread[i] = value
            parts = []
            for j in PLACES:
                first, last = (
                    jnp.broadcast_to(spread[i, 2 * j + e : 2 * j + e + 1, :], (ROWS, LANES))
                    for e in (0, 1)
                )
                parts.append(
                    jnp.where(sublane == 0, first, jnp.where(sublane == ROWS - 1, last, 0.0))
                )
            out.append(jnp.stack(parts))
        return out

    def with_ring(sums, ring):
        return tuple(t + r for t, r in zip(sums, unring(ring_sums(ring))))

    zero = jnp.zeros((blocks, ROWS, LANES), f32)

    arrive(rim1)
    duplicate_rim(own1, range(4))
    drain = weigh(True, own1)
    centre(own1)
    ring_masks()
    for plane in range(3):
        ring_centre(plane, lambda k, r: own1[plane, k, r : r + 1, :])
    for m in range(2):
        ring_centre(3 + m, lambda k, r: here_inv[m, k, r : r + 1, :])
    sums = evaluate(True, own1, (zero,) * 3)
    local[5].wait()
    velocity = [jnp.stack(cut(vel_v[i])) for i in range(2)]

    arrive(kinds_far)
    unpack(far1, 4, 0)
    drain = drain + weigh(False, far1)
    drain = drain + unring([ring_weigh()])[0]
    arrive(fields_far)
    ring_fields(ring1, far1)
    moving, after = [], []
    for outs in (ALL,):
        span = slice(outs[0], outs[-1] + 1)
        part = with_ring(evaluate(False, far1, sums), ring1)
        new = finish(own1, part, drain[span], [t[span] for t in velocity], outs)
        for plane in range(3):
            own2[plane, span, 0:ROWS, :] = new[plane]
            own2[plane, span, ROWS : 2 * ROWS, :] = new[plane]
        after.append(new[3:])
        moving += send_straight(own2, far2, fields, pl.ds(outs[0], len(outs)))
        if True:
            pack(own2, 3, 1)
            moving += send_corners(1)
            rim2 = send_across(own2)
    velocity = [jnp.concatenate(pair, axis=0) for pair in zip(*after)]

    arrive(rim2)
    duplicate_rim(own2, range(3))
    centre(own2)
    sums = evaluate(True, own2, (zero,) * 3)
    sums = evaluate(False, None, sums, ends="near")
    for plane in range(3):
        ring_centre(plane, lambda k, r: own2[plane, k, r : r + 1, :])
    finish_sends(7)
    arrive(moving)
    unpack(far2, 3, 1)
    ring_fields(ring2, far2)
    sums = evaluate(False, far2, sums, ends="far")
    sums = with_ring(sums, ring2)
    n0, n1, np_, v0, v1 = finish(own2, sums, drain, velocity)

    for k, j in enumerate(PLACES):
        at = slice(j * LANES, (j + 1) * LANES)
        out_disp[0, :, at] = n0[k]
        out_disp[1, :, at] = n1[k]
        out_vel[0, :, at] = v0[k]
        out_vel[1, :, at] = v1[k]
        out_pres[:, at] = np_[k]

    finish_sends(len(messages))


def hand_over(a, b, c, out_a, out_b, out_c, sems):
    copies = [
        pltpu.make_async_copy(source, target, sems.at[i])
        for i, (source, target) in enumerate(((a, out_a), (b, out_b), (c, out_c)))
    ]
    for copy in copies:
        copy.start()
    for copy in copies:
        copy.wait()


def body(gx_count, displacement, velocity, pressure, broken_bits, material_class, table):
    height, breadth = pressure.shape
    assert height == ROWS and breadth % LANES == 0 and breadth == len(PLACES) * LANES
    blocks = breadth // LANES
    vmem = pl.BlockSpec(memory_space=pltpu.VMEM)
    anywhere = pl.BlockSpec(memory_space=pltpu.HBM)
    f, i32 = jnp.float32, jnp.int32
    dma = pltpu.SemaphoreType.DMA
    n_own, n_far = (len(SLOTS[own]) for own in (True, False))

    def planes(n, blocks, rows):
        return pltpu.VMEM((n, blocks, rows, LANES), f)

    shapes = (displacement.shape, velocity.shape, pressure.shape)
    results = pl.pallas_call(
        functools.partial(kernel, gx_count),
        out_shape=tuple(pltpu.VMEM(s, f) for s in shapes),
        in_specs=[anywhere] * 6,
        out_specs=(vmem, vmem, vmem),
        scratch_shapes=[
            pltpu.VMEM(displacement.shape, f),
            pltpu.VMEM(velocity.shape, f),
            pltpu.VMEM(pressure.shape, f),
            pltpu.VMEM(broken_bits.shape, i32),
            pltpu.VMEM(material_class.shape, i32),
            pltpu.SMEM(table.shape, f),
            planes(4, blocks + 1, 2 * ROWS),
            planes(4, blocks + 1, 2 * ROWS),
            planes(3, blocks + 1, 2 * ROWS),
            planes(3, blocks + 1, 2 * ROWS),
            pltpu.VMEM((2, ROWS, LANES), f),
            pltpu.VMEM((2, 2 * ROWS, LANES), f),
            planes(SPAN, blocks + 1, 2 * ROWS),
            planes(SPAN, blocks + 1, 2 * ROWS),
            planes(SPAN, blocks, 2 * ROWS),
            planes(SPAN, blocks, 2 * ROWS),
            pltpu.VMEM((2, SPAN, blocks, 2 * ROWS, LANES), f),
            pltpu.VMEM((2, SPAN, blocks, 2 * ROWS, LANES), f),
            planes(2, table.shape[0], ROWS),
            planes(2, blocks, ROWS),
            planes(n_own, blocks, ROWS),
            planes(n_own, blocks, ROWS),
            planes(n_far, blocks, ROWS),
            planes(n_far, blocks, ROWS),
            planes(n_own, blocks, ROWS),
            planes(n_far, blocks, ROWS),
            planes(Y_SLOTS, blocks + 1, ROWS),
            planes(Y_SLOTS, blocks + 1, ROWS),
            planes(SPAN, blocks, ROWS),
            planes(2, blocks, ROWS),
            pltpu.VMEM((5, RING, LANES), f),
            pltpu.VMEM((5, RING, LANES), f),
            pltpu.VMEM((5, ROWS, LANES), f),
            pltpu.VMEM((SPAN, ROWS, LANES), f),
            pltpu.VMEM((SPAN, ROWS, LANES), f),
            pltpu.VMEM((3, ROWS, LANES), f),
            dma((6,)), dma((MESSAGES,)), dma((MESSAGES,)),
        ],
        compiler_params=pltpu.CompilerParams(
            collective_id=0, has_side_effects=True, vmem_limit_bytes=62 * 1024 * 1024
        ),
        name="peridynamics",
    )(displacement, velocity, pressure, broken_bits, material_class, table)
    return pl.pallas_call(
        hand_over,
        out_shape=tuple(jax.ShapeDtypeStruct(s, f) for s in shapes),
        in_specs=[vmem] * 3,
        out_specs=(anywhere,) * 3,
        scratch_shapes=[dma((3,))],
        name="hand_over",
    )(*[pltpu.with_memory_space_constraint(r, pltpu.VMEM) for r in results])


def solution(mesh):
    plane = P(("sample", "gx"), "gy")
    stack = P(None, ("sample", "gx"), "gy")
    assert mesh.shape["gy"] == 2
    return jax.shard_map(
        functools.partial(body, mesh.shape["gx"]),
        mesh=mesh,
        in_specs=(stack, stack, plane, stack, plane, P("sample", None)),
        out_specs=(stack, stack, plane),
        check_vma=False,
    )
```

```python
import functools
import math

import jax
import jax.numpy as jnp
from jax import lax
from jax.experimental import pallas as pl
from jax.experimental.pallas import tpu as pltpu
from jax.sharding import PartitionSpec as P

REACH = 6
SPAN = 2 * REACH + 1
MESH = pl.DeviceIdType.MESH
LANES = 128
ROWS = 8
OUTSIDE = -1
PLACES = (0, 3, 1, 2)
RIM = len(PLACES)
AFTER, BEFORE = (2, RIM, 3, 1), (RIM, 3, 0, 2)
OUTER, INNER, ALL = (0, 1), (2, 3), (0, 1, 2, 3)
MESSAGES = 12
STRIP = 16
HALF = 4
JOINED = (2, 3)
Y_SLOTS = ROWS + 3
FAR = 3.0e38

half_width = {a: math.isqrt(37 - a * a) for a in range(-REACH, REACH + 1)}
first_bond = {}
_count = 0
for _a in range(-REACH, REACH + 1):
    first_bond[_a] = _count
    _count += 2 * half_width[_a] + 1 - (1 if _a == 0 else 0)


def bond(a, b):
    if abs(a) > REACH or abs(b) > half_width[a] or (a == 0 and b == 0):
        return None
    return first_bond[a] + b + half_width[a] - (1 if a == 0 and b > 0 else 0)


def groups_of(own):
    offsets = range(ROWS) if own else range(2, ROWS - 1)
    out = [(o, o, o - ROWS if o else 0) if own else (o, o - ROWS, o) for o in offsets]
    return out if own else out + [(-m, -m, m) for m in JOINED]


RING = 16


def columns_of(low, high):
    return max(half_width.get(low, -1), half_width.get(high, -1))


def slots_of(own):
    slots = {}
    for o, low, high in groups_of(own):
        widths = half_width.get(low, -1), half_width.get(high, -1)
        for b in range(-max(widths), max(widths) + 1):
            one_sided = abs(b) > min(widths)
            if not own and o > 0 and one_sided:
                continue
            if o < 0 and abs(b) <= half_width.get(ROWS + o, -1):
                continue
            if low or b:
                slots[o, b] = len(slots)
    return slots


SLOTS = {own: slots_of(own) for own in (True, False)}


def kernel(
    gx_count, disp, vel, pres, bits, klass, table,
    out_disp, out_vel, out_pres,
    disp_v, vel_v, pres_v, bits_v, klass_v, table_s,
    own1, far1, own2, far2, own_pack, far_pack,
    z_own, z_far, q_own, q_far, inv_own, inv_far, inverse, here_inv,
    w_own, v_own, w_far, v_far, ex_own, ex_far, y_own, y_far, side_b, still,
    ring1, ring2, ring_here, w_ring, v_ring, spread,
    local_sem, send_sem, recv_sem,
):
    f32 = jnp.float32
    sample, gx, gy = lax.axis_index("sample"), lax.axis_index("gx"), lax.axis_index("gy")
    height, breadth = pres.shape
    blocks = breadth // LANES
    has_up, has_down = gx > 0, gx < gx_count - 1
    up, down, mate = gx - 1, gx + 1, 1 - gy

    barrier = pltpu.get_barrier_semaphore()

    def greet(x, y):
        pl.semaphore_signal(barrier, inc=1, device_id=(sample, x, y), device_id_type=MESH)

    @pl.when(has_up)
    def _():
        greet(up, gy)
        greet(up, mate)

    @pl.when(has_down)
    def _():
        greet(down, gy)
        greet(down, mate)

    greet(gx, mate)

    local = [
        pltpu.make_async_copy(table, table_s, local_sem.at[0]),
        pltpu.make_async_copy(klass, klass_v, local_sem.at[1]),
        pltpu.make_async_copy(disp, disp_v, local_sem.at[2]),
        pltpu.make_async_copy(pres, pres_v, local_sem.at[3]),
        pltpu.make_async_copy(bits, bits_v, local_sem.at[4]),
        pltpu.make_async_copy(vel, vel_v, local_sem.at[5]),
    ]
    for copy in local:
        copy.start()

    def clear(rows):
        count = rows.stop - rows.start
        for ref, planes in ((far1, 4), (far2, 3)):
            for plane in range(planes):
                fill = float(OUTSIDE) if plane == 3 else 0.0
                ref[plane, :blocks, rows, :] = jnp.full((blocks, count, LANES), fill, f32)
        far_pack[:, rows, :] = jnp.full((2, count, LANES), float(OUTSIDE), f32)

    clear(slice(0, ROWS - REACH))
    clear(slice(ROWS + REACH, 2 * ROWS))

    @pl.when(jnp.logical_not(has_up))
    def _():
        clear(slice(ROWS - REACH, ROWS))

    @pl.when(jnp.logical_not(has_down))
    def _():
        clear(slice(ROWS, ROWS + REACH))


    def cut(value):
        return [value[:, j * LANES : (j + 1) * LANES] for j in PLACES]

    def put(target, plane, value):
        for j, piece in enumerate(cut(value)):
            for rows in (slice(0, ROWS), slice(ROWS, 2 * ROWS)):
                target[plane, j, rows, :] = piece

    for i in (1, 2, 3):
        local[i].wait()
    put(own1, 3, klass_v[...].astype(f32))
    put(own1, 0, disp_v[0])
    put(own1, 1, disp_v[1])
    put(own1, 2, pres_v[...])

    edge, rim = pl.ds(1 - gy, 1), pl.ds(RIM, 1)
    to_up = (pl.ds(0, REACH), pl.ds(ROWS, REACH))
    to_down = (pl.ds(ROWS - REACH, REACH), pl.ds(ROWS - REACH, REACH))
    routes = (
        (has_up, has_down, (sample, up, gy), to_up),
        (has_down, has_up, (sample, down, gy), to_down),
        (has_up, has_down, (sample, up, mate), to_up),
        (has_down, has_up, (sample, down, mate), to_down),
        (None, None, (sample, gx, mate), None),
    )
    STRAIGHT, CORNERS, ACROSS = (0, 1), (2, 3), (4,)
    messages = []

    def when(condition, act):
        if condition is None:
            act()
        else:
            pl.when(condition)(act)

    sublane = lax.broadcasted_iota(jnp.int32, (ROWS, LANES), 0)
    lane = lax.broadcasted_iota(jnp.int32, (ROWS, LANES), 1)

    def pack(x, planes, which):
        strip = ((lane - (1 - gy) * (LANES - STRIP)) & (LANES - 1)) >> 4
        total = None
        for plane in range(planes):
            value = x[plane, pl.ds(1 - gy, 1), 0:ROWS, :][0]
            if plane:
                total = jnp.where(strip == plane, pltpu.roll(value, STRIP * plane, 1), total)
            else:
                total = value
        own_pack[which] = total

    def unpack(x, planes, which):
        for rows in (slice(0, ROWS), slice(ROWS, 2 * ROWS)):
            value = far_pack[which, rows, :]
            for plane in range(planes):
                x[plane, RIM, rows, :] = (
                    pltpu.roll(value, LANES - STRIP * plane, 1) if plane else value
                )

    def send(routes_used, source, target):
        sent = []
        for n in routes_used:
            going, coming, device, rows = routes[n]
            here, there = (pl.ds(0, ROWS),) * 2 if rows is None else rows
            m = len(messages)
            copy = pltpu.make_async_remote_copy(
                src_ref=source(here), dst_ref=target(there),
                send_sem=send_sem.at[m], recv_sem=recv_sem.at[m],
                device_id=device, device_id_type=MESH,
            )
            when(going, copy.start)
            messages.append((going, copy))
            sent.append((coming, copy))
        return sent

    def send_straight(own, far, planes, blocks):
        return send(
            STRAIGHT, lambda r: own.at[planes, blocks, r], lambda r: far.at[planes, blocks, r]
        )

    def send_across(own):
        return send(ACROSS, lambda r: own.at[:, edge, r], lambda r: own.at[:, rim, r])

    def send_corners(which):
        return send(CORNERS, lambda r: own_pack.at[which, r], lambda r: far_pack.at[which, r])

    waited = []

    def finish_sends(count):
        for going, copy in messages[len(waited) : count]:
            when(going, copy.wait_send)
            waited.append(copy)

    def arrive(sent):
        for coming, copy in sent:
            when(coming, copy.wait_recv)

    pack(own1, 4, 0)
    pl.semaphore_wait(
        barrier, 1 + 2 * has_up.astype(jnp.int32) + 2 * has_down.astype(jnp.int32)
    )
    fields, kinds = pl.ds(0, 3), pl.ds(3, 1)
    four = pl.ds(0, blocks)
    four = pl.ds(0, blocks)
    kinds_far = send_straight(own1, far1, kinds, four) + send_corners(0)
    fields_far = send_straight(own1, far1, fields, four)
    rim1 = send_across(own1)

    def first_rows(o):
        return sublane < (ROWS - o if o >= 0 else -o)

    def mix(o, low, high, kind=f32):
        return kind(low) if low == high else jnp.where(first_rows(o), kind(low), kind(high))

    def window(get, o):
        if o >= 0:
            return get(pl.ds(o, ROWS))
        return jnp.where(first_rows(o), get(pl.ds(ROWS + o, ROWS)), get(pl.ds(-o, ROWS)))

    local[0].wait()

    def look_up(which, member):
        value = jnp.full(which.shape, table_s[table.shape[0] - 1, member], f32)
        for c in range(table.shape[0] - 1):
            value = jnp.where(which == c, table_s[c, member], value)
        return value

    classes = table.shape[0]
    for m in range(2):
        for c in range(classes):
            inverse[m, c] = 1.0 / jnp.full((ROWS, LANES), table_s[c, m], f32)

    def inverses(which):
        out = [jnp.full(which.shape, FAR, f32)] * 2
        for c in range(classes):
            chosen = which == float(c)
            out = [jnp.where(chosen, inverse[m, c], out[m]) for m in range(2)]
        return out

    for m, value in enumerate(inverses(own1[3, :blocks, 0:ROWS, :])):
        here_inv[m] = value

    klass_own = klass_v[...]
    for plane, member in ((0, 2), (1, 3)):
        for j, piece in enumerate(cut(look_up(klass_own, member))):
            still[plane, j] = piece
    local[4].wait()
    for j in range(blocks):
        words = [bits_v[w, :, PLACES[j] * LANES : (PLACES[j] + 1) * LANES] for w in range(bits.shape[0])]

        def broken(a, b):
            k = bond(a, b)
            return jnp.int32(1) if k is None else words[k // 12] & (1 << (k % 12))

        for own, w_to, v_to in ((True, w_own, v_own), (False, w_far, v_far)):
            for o, low, high in groups_of(own):
                for b in range(-columns_of(low, high), columns_of(low, high) + 1):
                    if (o, b) not in SLOTS[own]:
                        continue
                    n = SLOTS[own][o, b]
                    one = broken(low, b)
                    if low != high:
                        one = jnp.where(first_rows(o), one, broken(high, b))
                    if o < 0:
                        one = jnp.where((sublane >= -o) & (sublane < ROWS + o), 1, one)
                    squares = [a * a + b * b for a in (low, high)]
                    w_to[n, j] = jnp.where(one == 0, mix(o, *[2.0 / x**2 for x in squares]), 0.0)
                    v_to[n, j] = jnp.where(one == 0, mix(o, *[2.0 / x for x in squares]), 0.0)

    def load(get, which):
        runs = []
        for k in which:
            if runs and runs[-1][1] == k:
                runs[-1][1] = k + 1
            else:
                runs.append([k, k + 1])
        pieces = [get(*run) for run in runs]
        return pieces[0] if len(pieces) == 1 else jnp.concatenate(pieces, axis=0)

    def shift(get, b, outs=ALL):
        if b == 0:
            return load(get, outs)
        other = [(AFTER if b > 0 else BEFORE)[k] for k in outs]
        sources = sorted(set(outs) | set(other))
        turned = pltpu.roll(load(get, sources), (-b) % LANES, 2)

        def take(which):
            at = [sources.index(k) for k in which]
            return load(lambda i, j: turned[i:j], at)

        return jnp.where(lane < LANES - b if b > 0 else lane >= -b, take(outs), take(other))

    def tiles(own):
        top, bottom = slice(0, ROWS), slice(ROWS, 2 * ROWS)
        return [(top, (top, bottom))] if own else [(top, (top,)), (bottom, (bottom,))]

    valid = (lane < LANES // 2) == (gy == 0)

    def weigh(own, x):
        w_ref, v_ref, inv = (w_own, v_own, inv_own) if own else (w_far, v_far, inv_far)
        known = []
        for read, write in tiles(own):
            value = x[3, :, read, :]
            rim_value = jnp.where(valid, value[blocks:], float(OUTSIDE))
            known.append(inverses(jnp.concatenate([value[:blocks], rim_value], axis=0)))
        if not own:
            for m in range(2):
                top, bottom = known[0][m], known[1][m]
                for i, k in enumerate(spots):
                    at = slice(2 * i, 2 * i + 1)
                    ring1[3 + m, at, :] = top[k, ROWS - 1 : ROWS]
                    ring1[3 + m, 2 * i + 1 : 2 * i + 2, :] = bottom[k, 0:1]
        drain = jnp.zeros((blocks, ROWS, LANES), f32)
        for b in sorted(range(-REACH, REACH + 1), key=abs):
            for (read, write), pair in zip(tiles(own), known):
                for m, value in enumerate(pair):
                    moved = shift(lambda i, j: value[i:j], b)
                    for rows in write:
                        inv[m, b + REACH, :, rows, :] = moved
            for o, low, high in groups_of(own):
                if (o, b) not in SLOTS[own]:
                    continue
                n = SLOTS[own][o, b]
                cubes = [0.25 * math.sqrt(a * a + b * b) ** 3 for a in (low, high)]
                weight, flow = (
                    ref[n]
                    * pl.reciprocal(
                        here_inv[m] + window(lambda r: inv[m, b + REACH, :, r, :], o),
                        approx=True,
                    )
                    for m, ref in enumerate((w_ref, v_ref))
                )
                share = mix(o, *cubes) * weight
                w_ref[n] = weight
                v_ref[n] = flow - share
                drain = drain + (flow + share)
        return drain

    def centre(x):
        u, v, p = (x[plane, :blocks, 0:ROWS, :] for plane in range(3))
        for b in range(-REACH, REACH + 1):
            side_b[b + REACH] = float(b) * v + (0.25 * b * b) * p
        for own, target in ((True, ex_own), (False, ex_far)):
            for o, low, high in groups_of(own):
                here = mix(o, low, high) * u + mix(o, 0.25 * low * low, 0.25 * high * high) * p
                for b in range(-columns_of(low, high), columns_of(low, high) + 1):
                    if (o, b) in SLOTS[own]:
                        target[SLOTS[own][o, b]] = here if b == 0 else here + side_b[b + REACH]

    def evaluate(own, x, sums, outs=ALL, ready=False, ends="both"):
        w_ref, v_ref, ex, z, q_moved, y = (
            (w_own, v_own, ex_own, z_own, q_own, y_own)
            if own
            else (w_far, v_far, ex_far, z_far, q_far, y_far)
        )
        slots = SLOTS[own]
        force_x, force_y, gain = sums
        span = slice(outs[0], outs[-1] + 1)
        ready = ready or ends == "near"
        if not ready:
            for o, low, high in groups_of(own):
                if low:
                    u, q = (window(lambda r: x[m, :, r, :], o) for m in (0, 2))
                    y[o % Y_SLOTS] = (
                        mix(o, low, high) * u
                        - mix(o, 0.25 * low * low, 0.25 * high * high) * q
                    )
        groups = groups_of(own)
        sets = (groups,) if len(outs) < len(ALL) else (groups[: HALF], groups[HALF:])
        for chosen in sets:
            row_sums = {}
            for b in range(REACH + 1):
                if not ready and chosen is sets[0]:
                    for read, write in tiles(own):
                        if b:
                            v, q = x[1, :, read, :], x[2, :, read, :]
                            bv, bq = float(b) * v, (-0.25 * b * b) * q
                            for rows in write:
                                z[REACH + b, :, rows, :] = bq + bv
                                z[REACH - b, :, rows, :] = bq - bv
                        for c in (b, -b) if b else (0,):
                            moved = shift(lambda i, j: x[2, i:j, read, :], c)
                            for rows in write:
                                q_moved[c + REACH, :, rows, :] = moved
                side_sum = None
                for o, low, high in chosen:
                    if (o, b) not in slots:
                        continue
                    def one(c):
                        n = slots[o, c]

                        def there(i, j):
                            if c == 0:
                                return y[o % Y_SLOTS, i:j]
                            side = window(lambda r: z[c + REACH, i:j, r, :], o)
                            return side + y[o % Y_SLOTS, i:j] if low else side

                        if ends == "near":
                            return w_ref[n, span] * ex[n, span], None
                        far = shift(there, c, outs)
                        mag = w_ref[n, span] * (far - ex[n, span] if ends == "both" else far)
                        moved = window(lambda r: q_moved[c + REACH, span, r, :], o)
                        return mag, v_ref[n, span] * moved

                    def add(total, value):
                        return value if total is None else total + value

                    length = mix(o, *[math.sqrt(a * a + b * b) for a in (low, high)])
                    mag, flow = one(b)
                    if b:
                        mag2, flow2 = one(-b)
                        side_sum = add(side_sum, mag - mag2)
                        mag = mag + mag2
                    if low:
                        row_sums[o] = add(row_sums.get(o), mag)
                    if ends == "near":
                        gain = gain + length * mag
                        continue
                    gain = gain - length * mag + flow
                    if b:
                        gain = gain + flow2
                if side_sum is not None:
                    force_y = force_y - float(b) * side_sum if ends == "near" else force_y + float(b) * side_sum
            for o, low, high in chosen:
                if low:
                    part = mix(o, low, high) * row_sums[o]
                    force_x = force_x - part if ends == "near" else force_x + part
        return force_x, force_y, gain

    def duplicate_rim(x, planes):
        for plane in planes:
            x[plane, RIM, ROWS : 2 * ROWS, :] = x[plane, RIM, 0:ROWS, :]

    def finish(x, sums, drain, velocity, outs=ALL):
        span = slice(outs[0], outs[-1] + 1)
        force_x, force_y, gain = sums
        u0, u1, p = (x[plane, span, 0:ROWS, :] for plane in range(3))
        density, storage = still[0, span], still[1, span]
        v0 = velocity[0] + 0.1 * (density * force_x - 0.5 * velocity[0])
        v1 = velocity[1] + 0.1 * (density * force_y - 0.5 * velocity[1])
        pressure = p + 0.1 * storage * 0.1 * (gain - drain * p)
        return u0 + 0.1 * v0, u1 + 0.1 * v1, pressure, v0, v1

    spots = [RIM] + [PLACES.index(j) for j in range(blocks)] + [RIM]
    odd = (sublane & 1) == 1
    step_a = jnp.where(odd, 1.0, -1.0)

    def fill_ring(ring, plane, get):
        for i, k in enumerate(spots):
            ring[plane, 2 * i : 2 * i + 1, :] = get(k, ROWS - 1)
            ring[plane, 2 * i + 1 : 2 * i + 2, :] = get(k, ROWS)

    def ring_fields(ring, far):
        for plane in range(3):
            fill_ring(ring, plane, lambda k, r: far[plane, k, r : r + 1, :])

    def ring_centre(plane, get):
        for j in range(blocks):
            k = PLACES.index(j)
            ring_here[plane, 2 * j : 2 * j + 1, :] = get(k, 0)
            ring_here[plane, 2 * j + 1 : 2 * j + 2, :] = get(k, ROWS - 1)

    def ring_masks():
        for b in range(-REACH, REACH + 1):
            for ref, scale in ((w_ring, 2.0 / (1 + b * b) ** 2), (v_ring, 2.0 / (1 + b * b))):
                for j in range(blocks):
                    for i, (a, r) in enumerate(((-1, 0), (1, ROWS - 1))):
                        k = bond(a, b)
                        word = bits_v[k // 12, r : r + 1, j * LANES : (j + 1) * LANES]
                        ref[b + REACH, 2 * j + i : 2 * j + i + 1, :] = jnp.where(
                            (word & (1 << (k % 12))) == 0, scale, 0.0
                        )

    MAIN = pl.ds(2, ROWS)

    def ring_shift(get, b):
        if b == 0:
            return get(MAIN)
        other = pl.ds(4, ROWS) if b > 0 else pl.ds(0, ROWS)
        mine, next_to = (pltpu.roll(get(r), (-b) % LANES, 1) for r in (MAIN, other))
        return jnp.where(lane < LANES - b if b > 0 else lane >= -b, mine, next_to)

    def ring_weigh():
        drain = jnp.zeros((ROWS, LANES), f32)
        for b in range(-REACH, REACH + 1):
            weight, flow = (
                ref[b + REACH]
                * pl.reciprocal(
                    ring_here[3 + m] + ring_shift(lambda r: ring1[3 + m, r, :], b), approx=True
                )
                for m, ref in enumerate((w_ring, v_ring))
            )
            share = (0.25 * math.sqrt(1 + b * b) ** 3) * weight
            w_ring[b + REACH] = weight
            v_ring[b + REACH] = flow - share
            drain = drain + (flow + share)
        return drain

    def ring_sums(ring):
        u, v, p = (ring_here[plane] for plane in range(3))
        near = step_a * u + 0.25 * p
        force_x = force_y = gain = pull = jnp.zeros((ROWS, LANES), f32)
        for b in range(-REACH, REACH + 1):
            def there(r):
                value = step_a * ring[0, r, :] - (0.25 + 0.25 * b * b) * ring[2, r, :]
                return value + float(b) * ring[1, r, :] if b else value

            mine = near + (float(b) * v + (0.25 * b * b) * p) if b else near
            mag = w_ring[b + REACH] * (ring_shift(there, b) - mine)
            gain = gain + v_ring[b + REACH] * ring_shift(lambda r: ring[2, r, :], b)
            pull = pull + math.sqrt(1 + b * b) * mag
            force_x = force_x + mag
            force_y = force_y + float(b) * mag
        return step_a * force_x, force_y, gain - pull

    def unring(values):
        out = []
        for i, value in enumerate(values):
            spread[i] = value
            parts = []
            for j in PLACES:
                first, last = (
                    jnp.broadcast_to(spread[i, 2 * j + e : 2 * j + e + 1, :], (ROWS, LANES))
                    for e in (0, 1)
                )
                parts.append(
                    jnp.where(sublane == 0, first, jnp.where(sublane == ROWS - 1, last, 0.0))
                )
            out.append(jnp.stack(parts))
        return out

    def with_ring(sums, ring):
        return tuple(t + r for t, r in zip(sums, unring(ring_sums(ring))))

    zero = jnp.zeros((blocks, ROWS, LANES), f32)

    arrive(rim1)
    duplicate_rim(own1, range(4))
    drain = weigh(True, own1)
    centre(own1)
    ring_masks()
    for plane in range(3):
        ring_centre(plane, lambda k, r: own1[plane, k, r : r + 1, :])
    for m in range(2):
        ring_centre(3 + m, lambda k, r: here_inv[m, k, r : r + 1, :])
    sums = evaluate(True, own1, (zero,) * 3)
    local[5].wait()
    velocity = [jnp.stack(cut(vel_v[i])) for i in range(2)]

    arrive(kinds_far)
    unpack(far1, 4, 0)
    drain = drain + weigh(False, far1)
    drain = drain + unring([ring_weigh()])[0]
    arrive(fields_far)
    ring_fields(ring1, far1)
    moving, after = [], []
    for outs in (ALL,):
        span = slice(outs[0], outs[-1] + 1)
        part = with_ring(evaluate(False, far1, sums), ring1)
        new = finish(own1, part, drain[span], [t[span] for t in velocity], outs)
        for plane in range(3):
            own2[plane, span, 0:ROWS, :] = new[plane]
            own2[plane, span, ROWS : 2 * ROWS, :] = new[plane]
        after.append(new[3:])
        moving += send_straight(own2, far2, fields, pl.ds(outs[0], len(outs)))
        if True:
            pack(own2, 3, 1)
            moving += send_corners(1)
            rim2 = send_across(own2)
    velocity = [jnp.concatenate(pair, axis=0) for pair in zip(*after)]

    arrive(rim2)
    duplicate_rim(own2, range(3))
    centre(own2)
    sums = evaluate(True, own2, (zero,) * 3)
    sums = evaluate(False, None, sums, ends="near")
    for plane in range(3):
        ring_centre(plane, lambda k, r: own2[plane, k, r : r + 1, :])
    finish_sends(7)
    arrive(moving)
    unpack(far2, 3, 1)
    ring_fields(ring2, far2)
    sums = evaluate(False, far2, sums, ends="far")
    sums = with_ring(sums, ring2)
    n0, n1, np_, v0, v1 = finish(own2, sums, drain, velocity)

    for k, j in enumerate(PLACES):
        at = slice(j * LANES, (j + 1) * LANES)
        out_disp[0, :, at] = n0[k]
        out_disp[1, :, at] = n1[k]
        out_vel[0, :, at] = v0[k]
        out_vel[1, :, at] = v1[k]
        out_pres[:, at] = np_[k]

    finish_sends(len(messages))


def hand_over(a, b, c, out_a, out_b, out_c, sems):
    copies = [
        pltpu.make_async_copy(source, target, sems.at[i])
        for i, (source, target) in enumerate(((a, out_a), (b, out_b), (c, out_c)))
    ]
    for copy in copies:
        copy.start()
    for copy in copies:
        copy.wait()


def body(gx_count, displacement, velocity, pressure, broken_bits, material_class, table):
    height, breadth = pressure.shape
    assert height == ROWS and breadth % LANES == 0 and breadth == len(PLACES) * LANES
    blocks = breadth // LANES
    vmem = pl.BlockSpec(memory_space=pltpu.VMEM)
    anywhere = pl.BlockSpec(memory_space=pltpu.HBM)
    f, i32 = jnp.float32, jnp.int32
    dma = pltpu.SemaphoreType.DMA
    n_own, n_far = (len(SLOTS[own]) for own in (True, False))

    def planes(n, blocks, rows):
        return pltpu.VMEM((n, blocks, rows, LANES), f)

    shapes = (displacement.shape, velocity.shape, pressure.shape)
    results = pl.pallas_call(
        functools.partial(kernel, gx_count),
        out_shape=tuple(pltpu.VMEM(s, f) for s in shapes),
        in_specs=[anywhere] * 6,
        out_specs=(vmem, vmem, vmem),
        scratch_shapes=[
            pltpu.VMEM(displacement.shape, f),
            pltpu.VMEM(velocity.shape, f),
            pltpu.VMEM(pressure.shape, f),
            pltpu.VMEM(broken_bits.shape, i32),
            pltpu.VMEM(material_class.shape, i32),
            pltpu.SMEM(table.shape, f),
            planes(4, blocks + 1, 2 * ROWS),
            planes(4, blocks + 1, 2 * ROWS),
            planes(3, blocks + 1, 2 * ROWS),
            planes(3, blocks + 1, 2 * ROWS),
            pltpu.VMEM((2, ROWS, LANES), f),
            pltpu.VMEM((2, 2 * ROWS, LANES), f),
            planes(SPAN, blocks + 1, 2 * ROWS),
            planes(SPAN, blocks + 1, 2 * ROWS),
            planes(SPAN, blocks, 2 * ROWS),
            planes(SPAN, blocks, 2 * ROWS),
            pltpu.VMEM((2, SPAN, blocks, 2 * ROWS, LANES), f),
            pltpu.VMEM((2, SPAN, blocks, 2 * ROWS, LANES), f),
            planes(2, table.shape[0], ROWS),
            planes(2, blocks, ROWS),
            planes(n_own, blocks, ROWS),
            planes(n_own, blocks, ROWS),
            planes(n_far, blocks, ROWS),
            planes(n_far, blocks, ROWS),
            planes(n_own, blocks, ROWS),
            planes(n_far, blocks, ROWS),
            planes(Y_SLOTS, blocks + 1, ROWS),
            planes(Y_SLOTS, blocks + 1, ROWS),
            planes(SPAN, blocks, ROWS),
            planes(2, blocks, ROWS),
            pltpu.VMEM((5, RING, LANES), f),
            pltpu.VMEM((5, RING, LANES), f),
            pltpu.VMEM((5, ROWS, LANES), f),
            pltpu.VMEM((SPAN, ROWS, LANES), f),
            pltpu.VMEM((SPAN, ROWS, LANES), f),
            pltpu.VMEM((3, ROWS, LANES), f),
            dma((6,)), dma((MESSAGES,)), dma((MESSAGES,)),
        ],
        compiler_params=pltpu.CompilerParams(
            collective_id=0, has_side_effects=True, vmem_limit_bytes=62 * 1024 * 1024
        ),
        name="peridynamics",
    )(displacement, velocity, pressure, broken_bits, material_class, table)
    return pl.pallas_call(
        hand_over,
        out_shape=tuple(jax.ShapeDtypeStruct(s, f) for s in shapes),
        in_specs=[vmem] * 3,
        out_specs=(anywhere,) * 3,
        scratch_shapes=[dma((3,))],
        name="hand_over",
    )(*[pltpu.with_memory_space_constraint(r, pltpu.VMEM) for r in results])


def solution(mesh):
    plane = P(("sample", "gx"), "gy")
    stack = P(None, ("sample", "gx"), "gy")
    assert mesh.shape["gy"] == 2
    return jax.shard_map(
        functools.partial(body, mesh.shape["gx"]),
        mesh=mesh,
        in_specs=(stack, stack, plane, stack, plane, P("sample", None)),
        out_specs=(stack, stack, plane),
        check_vma=False,
    )
```
